128 devices in a mesh: date: 16 (over z_hi, x, core), strip: 8 (over z_lo, y).
Axes of the slice: x: 4, y: 4, z: 4 (z_hi: 2, z_lo: 2; z = z_hi * 2 + z_lo), core: 2. Of those that a mesh axis runs over, the one named last changes fastest.
Arguments:
- raw_slc: bfloat16 [128, 512, 2, 3840], P('date', 'strip'), may hold values from -6 to 6
- line_shift: int32 [128], P('date'), may hold values from -1 to 0
- line_phase: int32 [128], P('date'), may hold values from 0 to 15
- col_shift: int32 [128], P('date'), may hold values from -184 to 184
- col_phase: int32 [128], P('date'), may hold values from 0 to 15
- pair_lags: int32 [128, 4], P('date'), may hold values from 0 to 10, as said below
Outputs:
- coherence: float32 [128, 4, 2, 128, 192], P('date', None, None, 'strip')
The draws below stay inside these ranges and needn't reach their ends.
Inputs may be any that keep to these rules, and one draw needn't show every extreme that they name: `pair_lags`: each date names up to 4 distinct partner distances from 4 to 10, 0 marking an empty slot, with uneven numbers of partners per date; a date plus its distance is always a date of the stack.
All inputs are finite; a program needn't handle non-finite values.
Results may differ from the reference program's by a relative error of at most 0.0067.
Values may be sent and summed in bfloat16 or wider, within the bound.
A program may use at most 192 MiB of HBM per device.

```python
import jax
import jax.numpy as jnp
from jax import lax

COLS = 3840
TAPS = 8
PHASES = 16
PADC = 192
LOOK_A = 4
LOOK_R = 20
MINLAG = 4
MAXLAG = 10
SLOTS = 4
DATES = 128
LINES = 512


def draw_pair_lags(key, part):
    key = jax.random.fold_in(key, 11)
    key_order, key_count, key_force = jax.random.split(key, 3)
    option_count = MAXLAG - MINLAG + 1
    scores = jax.random.randint(key_order, (DATES, option_count), 0, 1 << 20) * option_count + jnp.arange(option_count)[None, :]
    order = jnp.argsort(scores, axis=1, stable=True)
    candidates = (MINLAG + order[:, :SLOTS]).astype(jnp.int32)
    forced_row = jax.random.randint(key_force, (), 0, DATES - MAXLAG)
    row_hit = jnp.arange(DATES)[:, None] == forced_row
    slot_ids = jnp.arange(SLOTS)[None, :]
    swapped = jnp.where(row_hit & (candidates == MAXLAG), candidates[:, :1], candidates)
    swapped = jnp.where(row_hit & (slot_ids == 0), MAXLAG, swapped)
    counts = jax.random.randint(key_count, (DATES, 1), 1, SLOTS + 1)
    valid = (slot_ids < counts) & (jnp.arange(DATES)[:, None] + swapped < DATES)
    return jnp.where(valid, swapped, 0).astype(jnp.int32)


def plant(result, stream_key, smallest, high):
    longest = result.shape.index(max(result.shape))
    spots = []
    for shift in (0, 1):
        where = [jax.random.randint(jax.random.fold_in(stream_key, axis), (), 0, length) for axis, length in enumerate(result.shape)]
        where[longest] = (where[longest] + shift) % result.shape[longest]
        spots.append(tuple(where))
    return result.at[spots[0]].set(smallest).at[spots[1]].set(high)


def shard_levels(rng, shape, shards, low, high):
    def one(axis_at, shards_of):
        draws = jax.random.uniform(jax.random.fold_in(jax.random.fold_in(rng, 6), axis_at), (shards_of,), jnp.float32, low / len(shards), high / len(shards))
        return jnp.repeat(jnp.exp(draws), shape[axis_at] // shards_of).reshape((-1,) + (1,) * (len(shape) - axis_at - 1))

    factor_of = one(*shards[0])
    for cut in shards[1:]:
        factor_of = factor_of * one(*cut)
    return factor_of


def noise(stream_key, shape, scale, reach, shards=(), held_as=jnp.bfloat16):
    drawn = jax.random.normal(stream_key, shape, jnp.float32) * scale
    if len(shards) > 0:
        drawn = shard_levels(stream_key, shape, shards, -0.22, 0.18) * drawn
    return jnp.clip(drawn, min=-reach, max=reach).astype(held_as)


def setup_inputs(seed: int = 0) -> dict:
    arg_keys = jax.random.split(jax.random.key(seed), 7)
    return {
        "raw_slc": noise(arg_keys[0], (DATES, LINES, 2, COLS), 1.0, 6.0, ((0, 16), (1, 8))),
        "line_shift": plant(jax.random.randint(arg_keys[1], (DATES,), -1, 1), jax.random.fold_in(arg_keys[1], 1), -1, 0).astype(jnp.int32),
        "line_phase": plant(jax.random.randint(arg_keys[2], (DATES,), 0, PHASES), jax.random.fold_in(arg_keys[2], 1), 0, PHASES - 1).astype(jnp.int32),
        "col_shift": plant(jax.random.randint(arg_keys[3], (DATES,), 8 - PADC, PADC - 7), jax.random.fold_in(arg_keys[3], 1), 8 - PADC, (PADC - 7) - 1).astype(jnp.int32),
        "col_phase": plant(jax.random.randint(arg_keys[4], (DATES,), 0, PHASES), jax.random.fold_in(arg_keys[4], 1), 0, PHASES - 1).astype(jnp.int32),
        "pair_lags": draw_pair_lags(jax.random.fold_in(arg_keys[6], 71), 0),
    }


EPSILON = 1e-06

def sinc_weights_table():
    phase = jnp.arange(PHASES, dtype=jnp.float32)[:, None] / PHASES
    taps = jnp.arange(TAPS, dtype=jnp.float32)[None, :] - (TAPS // 2 - 1)
    offset = taps - phase
    window = 0.5 + 0.5 * jnp.cos(jnp.pi * offset / (TAPS // 2 + 0.5))
    weights = jnp.sinc(offset) * window
    return (weights / lax.optimization_barrier(jnp.sum(weights, axis=1, keepdims=True))).astype(jnp.bfloat16)

def coregister(slab, line_off, line_ph, col_off, col_ph, sinc_weights):
    line_count = slab.shape[0]
    col_count = slab.shape[2]
    half_taps = TAPS // 2 - 1
    padded = jnp.pad(slab, ((TAPS // 2, TAPS // 2), (0, 0), (0, 0)))
    azimuth = jnp.zeros(slab.shape, jnp.float32)
    for tap_index in range(TAPS):
        start = (line_off + tap_index + TAPS // 2 - half_taps).astype(jnp.int32)
        piece = lax.dynamic_slice_in_dim(padded, start, line_count, 0)
        azimuth = azimuth + sinc_weights[line_ph, tap_index].astype(jnp.float32) * piece.astype(jnp.float32)
    azimuth = azimuth.astype(jnp.bfloat16)
    padded_cols = jnp.pad(azimuth, ((0, 0), (0, 0), (PADC, PADC)))
    ranged = jnp.zeros(slab.shape, jnp.float32)
    for tap_index in range(TAPS):
        start = (PADC + col_off + tap_index - half_taps).astype(jnp.int32)
        piece = lax.dynamic_slice_in_dim(padded_cols, start, col_count, 2)
        ranged = ranged + sinc_weights[col_ph, tap_index].astype(jnp.float32) * piece.astype(jnp.float32)
    return ranged.astype(jnp.bfloat16)

def looked(values):
    line_count, col_count = values.shape
    grouped = values.astype(jnp.float32).reshape(line_count // LOOK_A, LOOK_A, col_count // LOOK_R, LOOK_R)
    return lax.optimization_barrier(jnp.sum(grouped, axis=(1, 3)))

def reference(raw_slc, line_shift, line_phase, col_shift, col_phase, pair_lags):
    sinc_weights = sinc_weights_table()

    def coreg_date(date_index):
        return coregister(raw_slc[date_index], line_shift[date_index], line_phase[date_index], col_shift[date_index], col_phase[date_index], sinc_weights)

    def per_date(date_index):
        ref_float = coreg_date(date_index).astype(jnp.float32)
        power_ref = looked((ref_float[:, 0] ** 2 + ref_float[:, 1] ** 2).astype(jnp.bfloat16))
        results = []
        for slot_index in range(SLOTS):
            lag_value = pair_lags[date_index, slot_index]
            partner = (date_index + jnp.where(lag_value > 0, lag_value, 0)).astype(jnp.int32)
            other_float = coreg_date(partner).astype(jnp.float32)
            power_other = looked((other_float[:, 0] ** 2 + other_float[:, 1] ** 2).astype(jnp.bfloat16))
            re_part = ref_float[:, 0] * other_float[:, 0] + ref_float[:, 1] * other_float[:, 1]
            im_part = ref_float[:, 1] * other_float[:, 0] - ref_float[:, 0] * other_float[:, 1]
            looked_sum = jnp.stack([looked(re_part.astype(jnp.bfloat16)), looked(im_part.astype(jnp.bfloat16))])
            scale = jnp.sqrt(power_ref * power_other + EPSILON)
            results.append(jnp.where(lag_value > 0, looked_sum / scale, jnp.zeros_like(looked_sum)))
        return jnp.stack(results)
    return lax.map(per_date, jnp.arange(DATES, dtype=jnp.int32))
```

```python
import functools

import jax
import jax.numpy as jnp
import numpy as np
from jax import lax
from jax.experimental import pallas as pl
from jax.experimental.pallas import tpu as pltpu
from jax.sharding import PartitionSpec as P

TAPS = 8
PHASES = 16
LOOK_A = 4
LOOK_R = 20
MINLAG = 4
MAXLAG = 10
EPSILON = 1e-06

LAGS = MAXLAG - MINLAG + 1
DATES = 8
LINES = 64
COLS = 3840
TILES = COLS // 128
HALF = COLS // 2
HTILES = HALF // 128
LOOKS = HALF // LOOK_R
LROWS = LINES // LOOK_A
ROWS = 2 * LINES
EDGE = TAPS // 2
SRC = LINES + 2 * EDGE
MOVED = 5
OWN0 = MOVED
NEXT0 = OWN0 + 2 * DATES
IMAGES = NEXT0 + MOVED
UFIRST = MINLAG
UCOUNT = 2 * DATES + MOVED - UFIRST

BF = jnp.bfloat16
F32 = jnp.float32
MESH = pl.DeviceIdType.MESH


def sinc_table():
    phase = np.arange(PHASES)[:, None] / PHASES
    offset = np.arange(TAPS)[None, :] - (TAPS // 2 - 1) - phase
    weights = np.sinc(offset) * (0.5 + 0.5 * np.cos(np.pi * offset / (TAPS // 2 + 0.5)))
    weights = (weights / weights.sum(axis=1, keepdims=True)).astype(np.float32)
    return weights.astype(BF).astype(np.float32).reshape(-1)


def kernel(
    raw, line_shift, line_phase, col_shift, col_phase, lags, table,
    out,
    images, other, halo, src, azim, lhs, look, power, mine, theirs, back, send_back,
    load_sem, halo_send, halo_recv, pair_send, pair_recv, far_send, far_recv,
    res_send, res_recv, back_send, back_recv,
):
    d, s = lax.axis_index("date"), lax.axis_index("strip")
    n_date, n_strip = lax.axis_size("date"), lax.axis_size("strip")
    core = d % 2
    chip = d // 2
    has_next = chip < n_date // 2 - 1
    has_prev = chip > 0
    has_up = s > 0
    has_down = s < n_strip - 1
    partner = d + 1 - 2 * core
    far_ok = jnp.where(core == 0, has_prev, has_next)
    far_chip = jnp.where(core == 0, chip - 1, chip + 1)

    def place(i):
        return jnp.where(core == 0, i, DATES - 1 - i)

    def load_tile(i, slot, c):
        return pltpu.make_async_copy(
            raw.at[place(i), :, :, pl.ds(pl.multiple_of(c * 128, 128), 128)],
            src.at[slot, c, pl.ds(EDGE, LINES)],
            load_sem.at[slot],
        )

    def load_edges(i, slot, c, side):
        return pltpu.make_async_copy(
            halo.at[i, side, :, :, pl.ds(pl.multiple_of(c * 128, 128), 128)],
            src.at[slot, c, pl.ds(side * (EDGE + LINES), EDGE)],
            load_sem.at[slot],
        )

    def start_lines(i, slot):
        @pl.loop(0, TILES)
        def _(c):
            load_tile(i, slot, c).start()

    def start_edges(i, slot):
        @pl.loop(0, TILES)
        def _(c):
            load_edges(i, slot, c, 0).start()
            load_edges(i, slot, c, 1).start()

    start_lines(0, 0)

    barrier = pltpu.get_barrier_semaphore()
    peers = 0
    for step in (-2, -1, 1, 2):
        ok = (d + step >= 0) & (d + step < n_date)
        peers = peers + ok.astype(jnp.int32)

        @pl.when(ok)
        def _():
            pl.semaphore_signal(barrier, inc=1, device_id=(d + step, s), device_id_type=MESH)

    for step, ok in ((-1, has_up), (1, has_down)):
        peers = peers + ok.astype(jnp.int32)

        @pl.when(ok)
        def _():
            pl.semaphore_signal(barrier, inc=1, device_id=(d, s + step), device_id_type=MESH)

    pl.semaphore_wait(barrier, peers)

    def edge_copy(i, side):
        return pltpu.make_async_remote_copy(
            src_ref=raw.at[place(i), pl.ds((1 - side) * (LINES - EDGE), EDGE)],
            dst_ref=halo.at[i, side],
            send_sem=halo_send.at[i, side],
            recv_sem=halo_recv.at[i, side],
            device_id=(d, s + 1 - 2 * side),
            device_id_type=MESH,
        )

    @pl.loop(0, DATES)
    def _(i):
        @pl.when(has_down)
        def _():
            edge_copy(i, 0).start()

        @pl.when(has_up)
        def _():
            edge_copy(i, 1).start()

    @pl.when(jnp.logical_not(has_up))
    def _():
        @pl.loop(0, DATES)
        def _(i):
            halo[i, 0] = jnp.zeros((EDGE, 2, COLS), BF)

    @pl.when(jnp.logical_not(has_down))
    def _():
        @pl.loop(0, DATES)
        def _(i):
            halo[i, 1] = jnp.zeros((EDGE, 2, COLS), BF)

    for t in (0, 1, TILES + 2, TILES + 3, TILES + 4):
        azim[t] = jnp.zeros((ROWS, 128), BF)
    look_row = lax.broadcasted_iota(jnp.int32, (HALF, LOOKS), 0)
    look_col = lax.broadcasted_iota(jnp.int32, (HALF, LOOKS), 1) * LOOK_R
    look[...] = jnp.where(
        (look_row >= look_col) & (look_row < look_col + LOOK_R), 1.0, 0.0
    ).astype(BF)

    def edge_wait(i):
        @pl.when(has_up)
        def _():
            edge_copy(i, 0).wait_recv()

        @pl.when(has_down)
        def _():
            edge_copy(i, 1).wait_recv()

    def far_copy(i, half_own):
        at = jnp.where(core == 0, NEXT0 + i, OWN0 - 1 - i)
        target = 2 * far_chip + (core if half_own else 1 - core)
        return pltpu.make_async_remote_copy(
            src_ref=images.at[OWN0 + DATES * core + place(i)] if half_own else other.at[i],
            dst_ref=images.at[at],
            send_sem=far_send.at[i, 1 if half_own else 0],
            recv_sem=far_recv.at[core, i],
            device_id=(target, s),
            device_id_type=MESH,
        )

    def far_arrived(side, i):
        at = NEXT0 + i if side == 0 else OWN0 - 1 - i
        return pltpu.make_async_remote_copy(
            src_ref=images.at[at], dst_ref=images.at[at],
            send_sem=far_send.at[i, 0], recv_sem=far_recv.at[side, i],
            device_id=(partner, s), device_id_type=MESH,
        )

    def pair_copy(i):
        return pltpu.make_async_remote_copy(
            src_ref=other.at[i],
            dst_ref=images.at[OWN0 + DATES * core + place(i)],
            send_sem=pair_send.at[i],
            recv_sem=pair_recv.at[i],
            device_id=(partner, s),
            device_id_type=MESH,
        )

    out_row = lax.broadcasted_iota(jnp.int32, (ROWS, 2 * SRC), 0)
    src_row = lax.broadcasted_iota(jnp.int32, (ROWS, 2 * SRC), 1)
    within = out_row % LINES
    out_line = (within % LROWS) * LOOK_A + within // LROWS
    line_tap = jnp.where(src_row % 2 == out_row // LINES, src_row // 2 - out_line - 1, 1000)
    col_tap = lax.broadcasted_iota(jnp.int32, (256, 256), 0) - lax.broadcasted_iota(
        jnp.int32, (256, 256), 1
    )

    edge_wait(0)
    start_edges(0, 0)

    @pl.loop(0, DATES)
    def _(i):
        slot = i % 2
        at = place(i)
        pltpu.make_async_copy(
            src.at[slot], src.at[slot], load_sem.at[slot]
        ).wait()

        @pl.when(i < DATES - 1)
        def _():
            start_lines(i + 1, 1 - slot)
            edge_wait(i + 1)
            start_edges(i + 1, 1 - slot)

        line_off, line_ph = line_shift[at], line_phase[at]
        col_off, col_ph = col_shift[at] - (TAPS // 2 - 1) + 256, col_phase[at]
        tile_off, rest = col_off // 128, col_off % 128
        line_band = jnp.zeros((ROWS, 2 * SRC), F32)
        band0 = jnp.zeros((256, 256), F32)
        band1 = jnp.zeros((144, 256), F32)
        for k in range(TAPS):
            line_band = jnp.where(line_tap - line_off == k, table[line_ph * TAPS + k], line_band)
            weight = table[col_ph * TAPS + k]
            band0 = jnp.where(col_tap - rest == k, weight, band0)
            band1 = jnp.where(col_tap[:144] + 256 - rest == k, weight, band1)
        line_band = line_band.astype(BF)
        col_band = jnp.concatenate([band0, band1], axis=0).astype(BF)

        for b in range(TILES // 2):
            block = jnp.concatenate(
                [src.at[slot, 2 * b + j].reshape(2 * SRC, 128)[...] for j in range(2)], axis=1
            )
            got = jnp.dot(line_band, block, preferred_element_type=F32).astype(BF)
            azim[2 * b + 2] = got[:, :128]
            azim[2 * b + 3] = got[:, 128:]

        def ranged(b):
            window = [azim[2 * b + j + tile_off] for j in range(4)]
            window[3] = window[3][:, :16]
            return jnp.dot(
                jnp.concatenate(window, axis=1), col_band, preferred_element_type=F32
            ).astype(BF)

        def put(t, value):
            lanes = pl.ds((t % HTILES) * 128, 128)
            first = t < HTILES

            @pl.when((core == 0) == first)
            def _():
                images[OWN0 + DATES * core + at, :, lanes] = value

            @pl.when((core == 0) != first)
            def _():
                other[i, :, lanes] = value

        for b in range(TILES // 2):
            got = ranged(b)
            put(2 * b, got[:, :128])
            put(2 * b + 1, got[:, 128:])

        @pl.when((i < MOVED) & far_ok)
        def _():
            far_copy(i, True).start()
            far_copy(i, False).start()

        pair_copy(i).start()

    def sums(x_at, others):
        count = len(others)

        @pl.loop(0, HTILES)
        def _(c):
            lanes = pl.ds(pl.multiple_of(c * 128, 128), 128)
            x = images[x_at, :, lanes]
            x0, x1 = x[:LINES], x[LINES:]

            def looked_lines(v):
                return (v[:LROWS] + v[LROWS : 2 * LROWS]) + (
                    v[2 * LROWS : 3 * LROWS] + v[3 * LROWS :]
                )

            lhs[pl.ds(0, LROWS), lanes] = looked_lines(x0 * x0 + x1 * x1)
            for n, y_at in enumerate(others):
                y = images[y_at, :, lanes]
                y0, y1 = y[:LINES], y[LINES:]
                row = LROWS * (1 + 2 * n)
                lhs[pl.ds(row, LROWS), lanes] = looked_lines(y0 * x0 + y1 * x1)
                lhs[pl.ds(row + LROWS, LROWS), lanes] = looked_lines(y1 * x0 - y0 * x1)

        total = jnp.dot(
            lhs[pl.ds(0, LROWS * (1 + 2 * count))], look[...], preferred_element_type=F32
        )
        here = total[:LROWS]
        power[x_at] = here
        results = []
        for n, y_at in enumerate(others):
            scale = 1.0 / jnp.sqrt(here * power[y_at] + EPSILON)
            row = LROWS * (1 + 2 * n)
            results.append((total[row : row + LROWS] * scale, total[row + LROWS : row + 2 * LROWS] * scale))
        return results

    def result_copy(u):
        return pltpu.make_async_remote_copy(
            src_ref=mine.at[u],
            dst_ref=theirs.at[u],
            send_sem=res_send.at[u],
            recv_sem=res_recv.at[u],
            device_id=(partner, s),
            device_id_type=MESH,
        )

    def later(u, first_lag, last_lag):
        x_at = OWN0 + u
        lag_list = list(range(first_lag, last_lag + 1))
        results = sums(x_at, [x_at - lag for lag in lag_list])
        for lag, (re_part, im_part) in zip(lag_list, results):
            mine[u - UFIRST, lag - MINLAG, 0] = re_part
            mine[u - UFIRST, lag - MINLAG, 1] = im_part
        result_copy(u - UFIRST).start()

    @pl.loop(0, DATES)
    def _(i):
        pair_copy(i).wait_recv()

    @pl.loop(0, MINLAG)
    def _(u):
        sums(OWN0 + u, [])

    for u in range(MINLAG, MAXLAG):
        later(u, MINLAG, u)

    @pl.loop(MAXLAG, 2 * DATES)
    def _(u):
        later(u, MINLAG, MAXLAG)

    def back_copy(i):
        return pltpu.make_async_remote_copy(
            src_ref=send_back.at[i],
            dst_ref=back.at[core, i],
            send_sem=back_send.at[i],
            recv_sem=back_recv.at[core, i],
            device_id=(2 * chip - 1, s),
            device_id_type=MESH,
        )

    for i in range(MOVED):
        @pl.when(has_next)
        def _():
            far_arrived(0, i).wait_recv()
            later(2 * DATES + i, max(MINLAG, i + 1), MAXLAG)

        @pl.when(has_prev)
        def _():
            far_arrived(1, i).wait_recv()
            results = sums(OWN0 - 1 - i, [OWN0 + u for u in range(MOVED, 2 * MOVED - i)])
            for n, (re_part, im_part) in enumerate(results):
                send_back[i, n, 0] = re_part
                send_back[i, n, 1] = -im_part
            back_copy(i).start()

    @pl.loop(0, 2 * DATES - UFIRST)
    def _(u):
        result_copy(u).wait_recv()

    @pl.when(has_next)
    def _():
        @pl.loop(2 * DATES - UFIRST, UCOUNT)
        def _(u):
            result_copy(u).wait_recv()

    def back_arrived(half, i):
        return pltpu.make_async_remote_copy(
            src_ref=send_back.at[i], dst_ref=back.at[half, i],
            send_sem=back_send.at[i], recv_sem=back_recv.at[half, i],
            device_id=(partner, s), device_id_type=MESH,
        )

    @pl.when(has_next & (core == 1))
    def _():
        for i in range(MOVED):
            back_arrived(0, i).wait_recv()
            back_arrived(1, i).wait_recv()

    @pl.loop(0, DATES)
    def _(j):
        t = DATES * core + j
        row = jnp.clip(2 * DATES - 1 - t, 0, MOVED - 1)
        for slot in range(4):
            lag = lags[j, slot]
            u = t + lag
            at = jnp.clip(u - UFIRST, 0, UCOUNT - 1)
            which = jnp.clip(lag - MINLAG, 0, LAGS - 1)
            far_at = jnp.clip(u - 2 * DATES - MOVED, 0, MOVED - 1)
            from_back = u >= 2 * DATES + MOVED
            for part in range(2):
                own, got = mine[at, which, part], theirs[at, which, part]
                left = jnp.where(core == 0, own, got)
                right = jnp.where(core == 0, got, own)
                left = jnp.where(from_back, back[0, row, far_at, part], left)
                right = jnp.where(from_back, back[1, row, far_at, part], right)
                value = jnp.concatenate([left, right], axis=1)
                out[j, slot, part] = jnp.where(lag > 0, value, 0.0)

    @pl.loop(0, DATES)
    def _(i):
        @pl.when(has_down)
        def _():
            edge_copy(i, 0).wait_send()

        @pl.when(has_up)
        def _():
            edge_copy(i, 1).wait_send()

        pair_copy(i).wait_send()

    @pl.when(far_ok)
    def _():
        @pl.loop(0, MOVED)
        def _(i):
            far_copy(i, True).wait_send()
            far_copy(i, False).wait_send()

    @pl.loop(0, 2 * DATES - UFIRST)
    def _(u):
        result_copy(u).wait_send()

    @pl.when(has_next)
    def _():
        @pl.loop(2 * DATES - UFIRST, UCOUNT)
        def _(u):
            result_copy(u).wait_send()

    @pl.when(has_prev)
    def _():
        @pl.loop(0, MOVED)
        def _(i):
            back_copy(i).wait_send()


def on_device(raw_slc, line_shift, line_phase, col_shift, col_phase, pair_lags):
    smem = pl.BlockSpec(memory_space=pltpu.SMEM)
    dma = pltpu.SemaphoreType.DMA
    part = (2, LROWS, LOOKS)
    return pl.pallas_call(
        kernel,
        out_shape=jax.ShapeDtypeStruct((DATES, 4, 2, LROWS, 2 * LOOKS), F32),
        in_specs=[pl.BlockSpec(memory_space=pl.ANY)] + [smem] * 6,
        out_specs=pl.BlockSpec(memory_space=pltpu.VMEM),
        scratch_shapes=[
            pltpu.VMEM((IMAGES, ROWS, HALF), BF),
            pltpu.VMEM((DATES, ROWS, HALF), BF),
            pltpu.VMEM((DATES, 2, EDGE, 2, COLS), BF),
            pltpu.VMEM((2, TILES, SRC, 2, 128), BF),
            pltpu.VMEM((TILES + 5, ROWS, 128), BF),
            pltpu.VMEM((LROWS * (1 + 2 * LAGS), HALF), BF),
            pltpu.VMEM((HALF, LOOKS), BF),
            pltpu.VMEM((IMAGES, LROWS, LOOKS), F32),
            pltpu.VMEM((UCOUNT, LAGS) + part, F32),
            pltpu.VMEM((UCOUNT, LAGS) + part, F32),
            pltpu.VMEM((2, MOVED, MOVED) + part, F32),
            pltpu.VMEM((MOVED, MOVED) + part, F32),
            dma((2,)),
            dma((DATES, 2)),
            dma((DATES, 2)),
            dma((DATES,)),
            dma((DATES,)),
            dma((MOVED, 2)),
            dma((2, MOVED)),
            dma((UCOUNT,)),
            dma((UCOUNT,)),
            dma((MOVED,)),
            dma((2, MOVED)),
        ],
        compiler_params=pltpu.CompilerParams(
            collective_id=0, has_side_effects=True, vmem_limit_bytes=56 * 1024 * 1024
        ),
        name="coherence_stack",
    )(raw_slc, line_shift, line_phase, col_shift, col_phase, pair_lags, jnp.asarray(sinc_table()))


def solution(mesh):
    return jax.shard_map(
        on_device,
        mesh=mesh,
        in_specs=(
            P("date", "strip", None, None),
            P("date"),
            P("date"),
            P("date"),
            P("date"),
            P("date", None),
        ),
        out_specs=P("date", None, None, "strip", None),
        check_vma=False,
    )
```

```python
import functools

import jax
import jax.numpy as jnp
import numpy as np
from jax import lax
from jax.experimental import pallas as pl
from jax.experimental.pallas import tpu as pltpu
from jax.sharding import PartitionSpec as P

TAPS = 8
PHASES = 16
LOOK_A = 4
LOOK_R = 20
MINLAG = 4
MAXLAG = 10
EPSILON = 1e-06

LAGS = MAXLAG - MINLAG + 1
DATES = 8
LINES = 64
COLS = 3840
TILES = COLS // 128
HALF = COLS // 2
HTILES = HALF // 128
LOOKS = HALF // LOOK_R
LROWS = LINES // LOOK_A
ROWS = 2 * LINES
EDGE = TAPS // 2
SRC = LINES + 2 * EDGE
MOVED = 5
OWN0 = MOVED
NEXT0 = OWN0 + 2 * DATES
IMAGES = NEXT0 + MOVED
RELAYED = (1, 2)
RELAYS = ((7, 14, 8), (7, 15, 9), (8, 0, 6), (8, 1, 7))
OTHER0 = IMAGES
UFIRST = MINLAG
UCOUNT = 2 * DATES + MOVED - UFIRST

BF = jnp.bfloat16
F32 = jnp.float32
MESH = pl.DeviceIdType.MESH


def sinc_table():
    phase = np.arange(PHASES)[:, None] / PHASES
    offset = np.arange(TAPS)[None, :] - (TAPS // 2 - 1) - phase
    weights = np.sinc(offset) * (0.5 + 0.5 * np.cos(np.pi * offset / (TAPS // 2 + 0.5)))
    weights = (weights / weights.sum(axis=1, keepdims=True)).astype(np.float32)
    return weights.astype(BF).astype(np.float32).reshape(-1)


def kernel(
    raw, line_shift, line_phase, col_shift, col_phase, lags, table,
    out,
    images, relay, halo, src, azim, lhs, look, power, mine, theirs, back, send_back,
    load_sem, halo_send, halo_recv, pair_send, pair_recv, far_send, far_recv,
    res_send, res_recv, back_send, back_recv, relay_send, relay_recv,
):
    d, s = lax.axis_index("date"), lax.axis_index("strip")
    n_date, n_strip = lax.axis_size("date"), lax.axis_size("strip")
    core = d % 2
    chip = d // 2
    has_next = chip < n_date // 2 - 1
    has_prev = chip > 0
    has_up = s > 0
    has_down = s < n_strip - 1
    partner = d + 1 - 2 * core
    far_ok = jnp.where(core == 0, has_prev, has_next)
    far_chip = jnp.where(core == 0, chip - 1, chip + 1)

    crossing = (d == 7) | (d == 8)
    relaying = (d < 2) | (d >= n_date - 2)
    across = (s + n_strip // 2) % n_strip

    def place(i):
        return jnp.where(core == 0, i, DATES - 1 - i)

    def load_tile(i, slot, c):
        return pltpu.make_async_copy(
            raw.at[place(i), :, :, pl.ds(pl.multiple_of(c * 128, 128), 128)],
            src.at[slot, c, pl.ds(EDGE, LINES)],
            load_sem.at[slot],
        )

    def load_edges(i, slot, c, side):
        return pltpu.make_async_copy(
            halo.at[i, side, :, :, pl.ds(pl.multiple_of(c * 128, 128), 128)],
            src.at[slot, c, pl.ds(side * (EDGE + LINES), EDGE)],
            load_sem.at[slot],
        )

    def start_lines(i, slot):
        @pl.loop(0, TILES)
        def _(c):
            load_tile(i, slot, c).start()

    def start_edges(i, slot):
        @pl.loop(0, TILES)
        def _(c):
            load_edges(i, slot, c, 0).start()
            load_edges(i, slot, c, 1).start()

    start_lines(0, 0)

    barrier = pltpu.get_barrier_semaphore()
    peers = 0
    for step in (-2, -1, 1, 2):
        ok = (d + step >= 0) & (d + step < n_date)
        peers = peers + ok.astype(jnp.int32)

        @pl.when(ok)
        def _():
            pl.semaphore_signal(barrier, inc=1, device_id=(d + step, s), device_id_type=MESH)

    for step, ok in ((-1, has_up), (1, has_down)):
        peers = peers + ok.astype(jnp.int32)

        @pl.when(ok)
        def _():
            pl.semaphore_signal(barrier, inc=1, device_id=(d, s + step), device_id_type=MESH)

    for a, b in sorted({(min(p), max(p)) for x, y, z in RELAYS for p in ((x, y), (y, z))}):
        for here, there in ((a, b), (b, a)):
            peers = peers + (d == here).astype(jnp.int32)

            @pl.when(d == here)
            def _():
                pl.semaphore_signal(barrier, inc=1, device_id=(there, across), device_id_type=MESH)

    pl.semaphore_wait(barrier, peers)

    def edge_copy(i, side):
        return pltpu.make_async_remote_copy(
            src_ref=raw.at[place(i), pl.ds((1 - side) * (LINES - EDGE), EDGE)],
            dst_ref=halo.at[i, side],
            send_sem=halo_send.at[i, side],
            recv_sem=halo_recv.at[i, side],
            device_id=(d, s + 1 - 2 * side),
            device_id_type=MESH,
        )

    def edge_start(i):
        @pl.when(has_down)
        def _():
            edge_copy(i, 0).start()

        @pl.when(has_up)
        def _():
            edge_copy(i, 1).start()

    edge_start(0)

    @pl.when(jnp.logical_not(has_up))
    def _():
        @pl.loop(0, DATES)
        def _(i):
            halo[i, 0] = jnp.zeros((EDGE, 2, COLS), BF)

    @pl.when(jnp.logical_not(has_down))
    def _():
        @pl.loop(0, DATES)
        def _(i):
            halo[i, 1] = jnp.zeros((EDGE, 2, COLS), BF)

    for t in (0, 1, TILES + 2, TILES + 3, TILES + 4):
        azim[t] = jnp.zeros((ROWS, 128), BF)
    look_row = lax.broadcasted_iota(jnp.int32, (HALF, LOOKS), 0)
    look_col = lax.broadcasted_iota(jnp.int32, (HALF, LOOKS), 1) * LOOK_R
    look[...] = jnp.where(
        (look_row >= look_col) & (look_row < look_col + LOOK_R), 1.0, 0.0
    ).astype(BF)

    def edge_wait(i):
        @pl.when(has_up)
        def _():
            edge_copy(i, 0).wait_recv()

        @pl.when(has_down)
        def _():
            edge_copy(i, 1).wait_recv()

    def half_place(i, half):
        return jnp.where(core == half, OWN0 + DATES * core + place(i), OTHER0 + i)

    def far_copy(i, half):
        return pltpu.make_async_remote_copy(
            src_ref=images.at[half_place(i, half)],
            dst_ref=images.at[jnp.where(core == 0, NEXT0 + i, OWN0 - 1 - i)],
            send_sem=far_send.at[i, half],
            recv_sem=far_recv.at[core, i],
            device_id=(2 * far_chip + half, s),
            device_id_type=MESH,
        )

    def relay_in(i, half):
        return pltpu.make_async_remote_copy(
            src_ref=images.at[half_place(i, half)],
            dst_ref=relay.at[i - RELAYED[0]],
            send_sem=far_send.at[i, half],
            recv_sem=relay_recv.at[i - RELAYED[0]],
            device_id=(jnp.where(d == 7, n_date - 2, 0) + half, across),
            device_id_type=MESH,
        )

    def relay_out(i):
        return pltpu.make_async_remote_copy(
            src_ref=relay.at[i - RELAYED[0]],
            dst_ref=images.at[jnp.where(d < 2, NEXT0 + i, OWN0 - 1 - i)],
            send_sem=relay_send.at[i - RELAYED[0]],
            recv_sem=far_recv.at[jnp.where(d < 2, 0, 1), i],
            device_id=(jnp.where(d < 2, d + 6, d - 6), across),
            device_id_type=MESH,
        )

    def pass_on(i):
        @pl.when(relaying)
        def _():
            relay_in(i, 0).wait_recv()
            relay_out(i).start()

    def far_start(i, half):
        relayed = crossing & (i >= RELAYED[0]) & (i <= RELAYED[-1])

        @pl.when((i < MOVED) & far_ok & jnp.logical_not(relayed))
        def _():
            far_copy(i, half).start()

        @pl.when(relayed)
        def _():
            relay_in(i, half).start()

    def far_arrived(side, i):
        at = NEXT0 + i if side == 0 else OWN0 - 1 - i
        return pltpu.make_async_remote_copy(
            src_ref=images.at[at], dst_ref=images.at[at],
            send_sem=far_send.at[i, 0], recv_sem=far_recv.at[side, i],
            device_id=(partner, s), device_id_type=MESH,
        )

    def pair_copy(i):
        return pltpu.make_async_remote_copy(
            src_ref=images.at[OTHER0 + i],
            dst_ref=images.at[OWN0 + DATES * core + place(i)],
            send_sem=pair_send.at[i],
            recv_sem=pair_recv.at[i],
            device_id=(partner, s),
            device_id_type=MESH,
        )

    out_row = lax.broadcasted_iota(jnp.int32, (ROWS, 2 * SRC), 0)
    src_row = lax.broadcasted_iota(jnp.int32, (ROWS, 2 * SRC), 1)
    within = out_row % LINES
    out_line = (within % LROWS) * LOOK_A + within // LROWS
    line_tap = jnp.where(src_row % 2 == out_row // LINES, src_row // 2 - out_line - 1, 1000)
    col_tap = lax.broadcasted_iota(jnp.int32, (256, 256), 0) - lax.broadcasted_iota(
        jnp.int32, (256, 256), 1
    )

    edge_start(1)
    edge_wait(0)
    start_edges(0, 0)

    @pl.loop(0, DATES)
    def _(i):
        slot = i % 2
        at = place(i)
        pltpu.make_async_copy(
            src.at[slot], src.at[slot], load_sem.at[slot]
        ).wait()

        @pl.when(i < DATES - 1)
        def _():
            start_lines(i + 1, 1 - slot)

        @pl.when(i < DATES - 2)
        def _():
            edge_start(i + 2)

        line_off, line_ph = line_shift[at], line_phase[at]
        col_off, col_ph = col_shift[at] - (TAPS // 2 - 1) + 256, col_phase[at]
        tile_off, rest = col_off // 128, col_off % 128
        line_band = jnp.zeros((ROWS, 2 * SRC), F32)
        band0 = jnp.zeros((256, 256), F32)
        band1 = jnp.zeros((144, 256), F32)
        for k in range(TAPS):
            line_band = jnp.where(line_tap - line_off == k, table[line_ph * TAPS + k], line_band)
            weight = table[col_ph * TAPS + k]
            band0 = jnp.where(col_tap - rest == k, weight, band0)
            band1 = jnp.where(col_tap[:144] + 256 - rest == k, weight, band1)
        line_band = line_band.astype(BF)
        col_band = jnp.concatenate([band0, band1], axis=0).astype(BF)

        for b in range(TILES // 2):
            block = jnp.concatenate(
                [src.at[slot, 2 * b + j].reshape(2 * SRC, 128)[...] for j in range(2)], axis=1
            )
            got = jnp.dot(line_band, block, preferred_element_type=F32).astype(BF)
            azim[2 * b + 2] = got[:, :128]
            azim[2 * b + 3] = got[:, 128:]

        @pl.when(i < DATES - 1)
        def _():
            edge_wait(i + 1)
            start_edges(i + 1, 1 - slot)

        def ranged(b):
            window = [azim[2 * b + j + tile_off] for j in range(4)]
            window[3] = window[3][:, :16]
            return jnp.dot(
                jnp.concatenate(window, axis=1), col_band, preferred_element_type=F32
            ).astype(BF)

        half_at = [half_place(i, half) for half in range(2)]

        def put(t, value):
            images[half_at[t // HTILES], :, pl.ds((t % HTILES) * 128, 128)] = value

        for b in range(TILES // 2):
            got = ranged(b)
            put(2 * b, got[:, :128])
            put(2 * b + 1, got[:, 128:])
            if 2 * b + 1 == HTILES:
                far_start(i, 0)
        far_start(i, 1)
        pair_copy(i).start()

    def sums(x_at, others):
        count = len(others)

        @pl.loop(0, HTILES)
        def _(c):
            lanes = pl.ds(pl.multiple_of(c * 128, 128), 128)
            x = images[x_at, :, lanes]
            x0, x1 = x[:LINES], x[LINES:]

            def looked_lines(v):
                return (v[:LROWS] + v[LROWS : 2 * LROWS]) + (
                    v[2 * LROWS : 3 * LROWS] + v[3 * LROWS :]
                )

            lhs[pl.ds(0, LROWS), lanes] = looked_lines(x0 * x0 + x1 * x1)
            for n, y_at in enumerate(others):
                y = images[y_at, :, lanes]
                y0, y1 = y[:LINES], y[LINES:]
                row = LROWS * (1 + 2 * n)
                lhs[pl.ds(row, LROWS), lanes] = looked_lines(y0 * x0 + y1 * x1)
                lhs[pl.ds(row + LROWS, LROWS), lanes] = looked_lines(y1 * x0 - y0 * x1)

        total = jnp.dot(
            lhs[pl.ds(0, LROWS * (1 + 2 * count))], look[...], preferred_element_type=F32
        )
        here = total[:LROWS]
        power[x_at] = here
        results = []
        for n, y_at in enumerate(others):
            scale = 1.0 / jnp.sqrt(here * power[y_at] + EPSILON)
            row = LROWS * (1 + 2 * n)
            results.append((total[row : row + LROWS] * scale, total[row + LROWS : row + 2 * LROWS] * scale))
        return results

    def result_copy(u):
        return pltpu.make_async_remote_copy(
            src_ref=mine.at[u],
            dst_ref=theirs.at[u],
            send_sem=res_send.at[u],
            recv_sem=res_recv.at[u],
            device_id=(partner, s),
            device_id_type=MESH,
        )

    def later(u, first_lag, last_lag):
        x_at = OWN0 + u
        lag_list = list(range(first_lag, last_lag + 1))
        results = sums(x_at, [x_at - lag for lag in lag_list])
        for lag, (re_part, im_part) in zip(lag_list, results):
            mine[u - UFIRST, lag - MINLAG, 0] = re_part
            mine[u - UFIRST, lag - MINLAG, 1] = im_part
        result_copy(u - UFIRST).start()

    @pl.loop(0, DATES)
    def _(i):
        pair_copy(i).wait_recv()

    pass_on(RELAYED[0])

    @pl.loop(0, MINLAG)
    def _(u):
        sums(OWN0 + u, [])

    for u in range(MINLAG, MAXLAG):
        later(u, MINLAG, u)

    for i in RELAYED[1:]:
        pass_on(i)

    @pl.loop(MAXLAG, 2 * DATES)
    def _(u):
        later(u, MINLAG, MAXLAG)

    def back_copy(i):
        return pltpu.make_async_remote_copy(
            src_ref=send_back.at[i, pl.ds(0, MOVED - i)],
            dst_ref=back.at[core, i, pl.ds(0, MOVED - i)],
            send_sem=back_send.at[i],
            recv_sem=back_recv.at[core, i],
            device_id=(2 * chip - 1, s),
            device_id_type=MESH,
        )

    for i in range(MOVED):
        @pl.when(has_prev)
        def _():
            far_arrived(1, i).wait_recv()
            results = sums(OWN0 - 1 - i, [OWN0 + u for u in range(MOVED, 2 * MOVED - i)])
            for n, (re_part, im_part) in enumerate(results):
                send_back[i, n, 0] = re_part.astype(BF)
                send_back[i, n, 1] = (-im_part).astype(BF)
            back_copy(i).start()

        @pl.when(has_next)
        def _():
            far_arrived(0, i).wait_recv()
            later(2 * DATES + i, max(MINLAG, i + 1), MAXLAG)

    @pl.loop(0, 2 * DATES - UFIRST)
    def _(u):
        result_copy(u).wait_recv()

    @pl.when(has_next)
    def _():
        @pl.loop(2 * DATES - UFIRST, UCOUNT)
        def _(u):
            result_copy(u).wait_recv()

    def back_arrived(half, i):
        return pltpu.make_async_remote_copy(
            src_ref=send_back.at[i, pl.ds(0, MOVED - i)],
            dst_ref=back.at[half, i, pl.ds(0, MOVED - i)],
            send_sem=back_send.at[i], recv_sem=back_recv.at[half, i],
            device_id=(partner, s), device_id_type=MESH,
        )

    @pl.when(has_next & (core == 1))
    def _():
        for i in range(MOVED):
            back_arrived(0, i).wait_recv()
            back_arrived(1, i).wait_recv()

    @pl.loop(0, DATES)
    def _(j):
        t = DATES * core + j
        row = jnp.clip(2 * DATES - 1 - t, 0, MOVED - 1)
        for slot in range(4):
            lag = lags[slot, j]
            u = t + lag
            at = jnp.clip(u - UFIRST, 0, UCOUNT - 1)
            which = jnp.clip(lag - MINLAG, 0, LAGS - 1)
            far_at = jnp.clip(u - 2 * DATES - MOVED, 0, MOVED - 1)
            from_back = u >= 2 * DATES + MOVED
            for part in range(2):
                own, got = mine[at, which, part], theirs[at, which, part]
                left = jnp.where(core == 0, own, got)
                right = jnp.where(core == 0, got, own)
                left = jnp.where(from_back, back[0, row, far_at, part].astype(F32), left)
                right = jnp.where(from_back, back[1, row, far_at, part].astype(F32), right)
                value = jnp.concatenate([left, right], axis=1)
                out[j, slot, part] = jnp.where(lag > 0, value, 0.0)

    @pl.loop(0, DATES)
    def _(i):
        @pl.when(has_down)
        def _():
            edge_copy(i, 0).wait_send()

        @pl.when(has_up)
        def _():
            edge_copy(i, 1).wait_send()

        pair_copy(i).wait_send()

    @pl.when(far_ok)
    def _():
        @pl.loop(0, MOVED)
        def _(i):
            far_copy(i, 0).wait_send()
            far_copy(i, 1).wait_send()

    @pl.loop(0, 2 * DATES - UFIRST)
    def _(u):
        result_copy(u).wait_send()

    @pl.when(has_next)
    def _():
        @pl.loop(2 * DATES - UFIRST, UCOUNT)
        def _(u):
            result_copy(u).wait_send()

    @pl.when(has_prev)
    def _():
        for i in range(MOVED):
            back_copy(i).wait_send()

    @pl.when(relaying)
    def _():
        for i in RELAYED:
            relay_out(i).wait_send()


def on_device(raw_slc, line_shift, line_phase, col_shift, col_phase, pair_lags):
    smem = pl.BlockSpec(memory_space=pltpu.SMEM)
    dma = pltpu.SemaphoreType.DMA
    part = (2, LROWS, LOOKS)
    return pl.pallas_call(
        kernel,
        out_shape=jax.ShapeDtypeStruct((DATES, 4, 2, LROWS, 2 * LOOKS), F32),
        in_specs=[pl.BlockSpec(memory_space=pl.ANY)] + [smem] * 6,
        out_specs=pl.BlockSpec(memory_space=pltpu.VMEM),
        scratch_shapes=[
            pltpu.VMEM((IMAGES + DATES, ROWS, HALF), BF),
            pltpu.VMEM((len(RELAYED), ROWS, HALF), BF),
            pltpu.VMEM((DATES, 2, EDGE, 2, COLS), BF),
            pltpu.VMEM((2, TILES, SRC, 2, 128), BF),
            pltpu.VMEM((TILES + 5, ROWS, 128), BF),
            pltpu.VMEM((LROWS * (1 + 2 * LAGS), HALF), BF),
            pltpu.VMEM((HALF, LOOKS), BF),
            pltpu.VMEM((IMAGES, LROWS, LOOKS), F32),
            pltpu.VMEM((UCOUNT, LAGS) + part, F32),
            pltpu.VMEM((UCOUNT, LAGS) + part, F32),
            pltpu.VMEM((2, MOVED, MOVED) + part, BF),
            pltpu.VMEM((MOVED, MOVED) + part, BF),
            dma((2,)),
            dma((DATES, 2)),
            dma((DATES, 2)),
            dma((DATES,)),
            dma((DATES,)),
            dma((MOVED, 2)),
            dma((2, MOVED)),
            dma((UCOUNT,)),
            dma((UCOUNT,)),
            dma((MOVED,)),
            dma((2, MOVED)),
            dma((len(RELAYED),)),
            dma((len(RELAYED),)),
        ],
        compiler_params=pltpu.CompilerParams(
            collective_id=0, has_side_effects=True, vmem_limit_bytes=56 * 1024 * 1024
        ),
        name="coherence_stack",
    )(raw_slc, line_shift, line_phase, col_shift, col_phase, pair_lags.T, jnp.asarray(sinc_table()))


def solution(mesh):
    return jax.shard_map(
        on_device,
        mesh=mesh,
        in_specs=(
            P("date", "strip", None, None),
            P("date"),
            P("date"),
            P("date"),
            P("date"),
            P("date", None),
        ),
        out_specs=P("date", None, None, "strip", None),
        check_vma=False,
    )
```

```python
import functools

import jax
import jax.numpy as jnp
import numpy as np
from jax import lax
from jax.experimental import pallas as pl
from jax.experimental.pallas import tpu as pltpu
from jax.sharding import PartitionSpec as P

TAPS = 8
PHASES = 16
LOOK_A = 4
LOOK_R = 20
MINLAG = 4
MAXLAG = 10
EPSILON = 1e-06

LAGS = MAXLAG - MINLAG + 1
DATES = 8
LINES = 64
COLS = 3840
TILES = COLS // 128
HALF = COLS // 2
HTILES = HALF // 128
LOOKS = HALF // LOOK_R
LROWS = LINES // LOOK_A
ROWS = 2 * LINES
EDGE = TAPS // 2
SRC = LINES + 2 * EDGE
MOVED = 5
OWN0 = MOVED
NEXT0 = OWN0 + 2 * DATES
IMAGES = NEXT0 + MOVED
RELAYED = (0, 1)
RELAYS = ((7, 14, 8), (7, 15, 9), (8, 0, 6), (8, 1, 7))
AHEAD = 4
PASS_AT = 8
OTHER0 = IMAGES
UFIRST = MINLAG
UCOUNT = 2 * DATES + MOVED - UFIRST

BF = jnp.bfloat16
F32 = jnp.float32
MESH = pl.DeviceIdType.MESH


def sinc_table():
    phase = np.arange(PHASES)[:, None] / PHASES
    offset = np.arange(TAPS)[None, :] - (TAPS // 2 - 1) - phase
    weights = np.sinc(offset) * (0.5 + 0.5 * np.cos(np.pi * offset / (TAPS // 2 + 0.5)))
    weights = (weights / weights.sum(axis=1, keepdims=True)).astype(np.float32)
    return weights.astype(BF).astype(np.float32).reshape(-1)


def kernel(
    raw, line_shift, line_phase, col_shift, col_phase, lags, table,
    out,
    images, relay, halo, far_raw, far_shift, far_phase, far_col_shift, far_col_phase, shifts,
    src, azim, lhs, look, power, mine, theirs, back, send_back,
    load_sem, halo_send, halo_recv, pair_send, pair_recv, far_send, far_recv,
    res_send, res_recv, back_send, back_recv, relay_send, relay_recv, raw_send, raw_recv,
):
    d, s = lax.axis_index("date"), lax.axis_index("strip")
    n_date, n_strip = lax.axis_size("date"), lax.axis_size("strip")
    core = d % 2
    chip = d // 2
    has_next = chip < n_date // 2 - 1
    has_prev = chip > 0
    has_up = s > 0
    has_down = s < n_strip - 1
    partner = d + 1 - 2 * core
    far_ok = jnp.where(core == 0, has_prev, has_next)
    far_chip = jnp.where(core == 0, chip - 1, chip + 1)

    crossing = (d == 7) | (d == 8)
    relaying = (d < 2) | (d >= n_date - 2)
    across = (s + n_strip // 2) % n_strip

    def place(i):
        return jnp.where(core == 0, i, DATES - 1 - i)

    far_device = jnp.where(core == 0, d - 1, d + 1)
    far_image = jnp.where(core == 0, OWN0 - 1, NEXT0)
    has_raw = far_ok & jnp.logical_not(crossing)
    partner_raw = jnp.where(core == 0, has_next & (chip != 3), has_prev & (chip != 4))

    def raw_copies():
        pairs = (
            (raw.at[place(0)], far_raw),
            (line_shift, far_shift),
            (line_phase, far_phase),
            (col_shift, far_col_shift),
            (col_phase, far_col_phase),
        )
        return [
            pltpu.make_async_remote_copy(
                src_ref=a, dst_ref=b, send_sem=raw_send.at[n], recv_sem=raw_recv.at[n],
                device_id=(far_device, s), device_id_type=MESH,
            )
            for n, (a, b) in enumerate(pairs)
        ]

    def load_tile(lines, slot, c):
        return pltpu.make_async_copy(
            lines.at[:, :, pl.ds(pl.multiple_of(c * 128, 128), 128)],
            src.at[slot, c, pl.ds(EDGE, LINES)],
            load_sem.at[slot],
        )

    def load_edges(i, slot, c, side):
        return pltpu.make_async_copy(
            halo.at[i, side, :, :, pl.ds(pl.multiple_of(c * 128, 128), 128)],
            src.at[slot, c, pl.ds(side * (EDGE + LINES), EDGE)],
            load_sem.at[slot],
        )

    def start_lines(lines, slot):
        @pl.loop(0, TILES)
        def _(c):
            load_tile(lines, slot, c).start()

    def start_edges(i, slot):
        @pl.loop(0, TILES)
        def _(c):
            load_edges(i, slot, c, 0).start()
            load_edges(i, slot, c, 1).start()

    start_lines(raw.at[place(0)], 0)

    barrier = pltpu.get_barrier_semaphore()
    peers = 0
    for step in (-2, -1, 1, 2):
        ok = (d + step >= 0) & (d + step < n_date)
        peers = peers + ok.astype(jnp.int32)

        @pl.when(ok)
        def _():
            pl.semaphore_signal(barrier, inc=1, device_id=(d + step, s), device_id_type=MESH)

    for step, ok in ((-1, has_up), (1, has_down)):
        peers = peers + ok.astype(jnp.int32)

        @pl.when(ok)
        def _():
            pl.semaphore_signal(barrier, inc=1, device_id=(d, s + step), device_id_type=MESH)

    for a, b in sorted({(min(p), max(p)) for x, y, z in RELAYS for p in ((x, y), (y, z))}):
        for here, there in ((a, b), (b, a)):
            peers = peers + (d == here).astype(jnp.int32)

            @pl.when(d == here)
            def _():
                pl.semaphore_signal(barrier, inc=1, device_id=(there, across), device_id_type=MESH)

    pl.semaphore_wait(barrier, peers)

    def edge_copy(lines, i, side):
        return pltpu.make_async_remote_copy(
            src_ref=halo.at[i, side] if lines is None else lines.at[
                pl.ds((1 - side) * (LINES - EDGE), EDGE)
            ],
            dst_ref=halo.at[i, side],
            send_sem=halo_send.at[i, side],
            recv_sem=halo_recv.at[i, side],
            device_id=(d, s + 1 - 2 * side),
            device_id_type=MESH,
        )

    def edge_start(lines, i):
        @pl.when(has_down)
        def _():
            edge_copy(lines, i, 0).start()

        @pl.when(has_up)
        def _():
            edge_copy(lines, i, 1).start()

    edge_start(raw.at[place(0)], 0)

    @pl.when(has_raw)
    def _():
        for copy in raw_copies():
            copy.start()

    @pl.when(jnp.logical_not(has_up))
    def _():
        @pl.loop(0, DATES + 1)
        def _(i):
            halo[i, 0] = jnp.zeros((EDGE, 2, COLS), BF)

    @pl.when(jnp.logical_not(has_down))
    def _():
        @pl.loop(0, DATES + 1)
        def _(i):
            halo[i, 1] = jnp.zeros((EDGE, 2, COLS), BF)

    for t in (0, 1, TILES + 2, TILES + 3, TILES + 4):
        azim[t] = jnp.zeros((ROWS, 128), BF)
    look_row = lax.broadcasted_iota(jnp.int32, (HALF, LOOKS), 0)
    look_col = lax.broadcasted_iota(jnp.int32, (HALF, LOOKS), 1) * LOOK_R
    look[...] = jnp.where(
        (look_row >= look_col) & (look_row < look_col + LOOK_R), 1.0, 0.0
    ).astype(BF)

    def edge_wait(i):
        @pl.when(has_up)
        def _():
            edge_copy(None, i, 0).wait_recv()

        @pl.when(has_down)
        def _():
            edge_copy(None, i, 1).wait_recv()

    def own_place(i):
        return jnp.where(i < DATES, OWN0 + DATES * core + place(i), far_image)

    def half_place(i, half):
        return jnp.where(core == half, own_place(i), OTHER0 + i)

    def far_copy(i, half):
        return pltpu.make_async_remote_copy(
            src_ref=images.at[half_place(i, half)],
            dst_ref=images.at[jnp.where(core == 0, NEXT0 + i, OWN0 - 1 - i)],
            send_sem=far_send.at[i, half],
            recv_sem=far_recv.at[core, i],
            device_id=(2 * far_chip + half, s),
            device_id_type=MESH,
        )

    def relay_in(i, half):
        return pltpu.make_async_remote_copy(
            src_ref=images.at[half_place(i, half)],
            dst_ref=relay.at[i - RELAYED[0]],
            send_sem=far_send.at[i, half],
            recv_sem=relay_recv.at[i - RELAYED[0]],
            device_id=(jnp.where(d == 7, n_date - 2, 0) + half, across),
            device_id_type=MESH,
        )

    def relay_out(i):
        return pltpu.make_async_remote_copy(
            src_ref=relay.at[i - RELAYED[0]],
            dst_ref=images.at[jnp.where(d < 2, NEXT0 + i, OWN0 - 1 - i)],
            send_sem=relay_send.at[i - RELAYED[0]],
            recv_sem=far_recv.at[jnp.where(d < 2, 0, 1), i],
            device_id=(jnp.where(d < 2, d + 6, d - 6), across),
            device_id_type=MESH,
        )

    def pass_on(i):
        @pl.when(relaying)
        def _():
            relay_in(i, 0).wait_recv()
            relay_out(i).start()

    def far_start(i, half):
        relayed = crossing & (i >= RELAYED[0]) & (i <= RELAYED[-1])

        direct = far_ok & (i < MOVED) & ((i > 0) | crossing) & jnp.logical_not(relayed)

        @pl.when(direct)
        def _():
            far_copy(i, half).start()

        @pl.when(relayed)
        def _():
            relay_in(i, half).start()

    def far_arrived(side, i):
        at = NEXT0 + i if side == 0 else OWN0 - 1 - i
        return pltpu.make_async_remote_copy(
            src_ref=images.at[at], dst_ref=images.at[at],
            send_sem=far_send.at[i, 0], recv_sem=far_recv.at[side, i],
            device_id=(partner, s), device_id_type=MESH,
        )

    def pair_copy(i):
        return pltpu.make_async_remote_copy(
            src_ref=images.at[OTHER0 + i],
            dst_ref=images.at[own_place(i)],
            send_sem=pair_send.at[i],
            recv_sem=pair_recv.at[i],
            device_id=(partner, s),
            device_id_type=MESH,
        )

    out_row = lax.broadcasted_iota(jnp.int32, (ROWS, 2 * SRC), 0)
    src_row = lax.broadcasted_iota(jnp.int32, (ROWS, 2 * SRC), 1)
    within = out_row % LINES
    out_line = (within % LROWS) * LOOK_A + within // LROWS
    line_tap = jnp.where(src_row % 2 == out_row // LINES, src_row // 2 - out_line - 1, 1000)
    col_tap = lax.broadcasted_iota(jnp.int32, (256, 256), 0) - lax.broadcasted_iota(
        jnp.int32, (256, 256), 1
    )

    for n in range(1, AHEAD):
        edge_start(raw.at[place(n)], n)
    edge_wait(0)
    start_edges(0, 0)

    count = DATES + has_raw.astype(jnp.int32)

    @pl.loop(0, count)
    def _(i):
        slot = i % 2
        at = jnp.where(i < DATES, place(i), jnp.where(core == 0, DATES - 1, 0))
        pltpu.make_async_copy(
            src.at[slot], src.at[slot], load_sem.at[slot]
        ).wait()

        @pl.when(i < DATES - 1)
        def _():
            start_lines(raw.at[place(i + 1)], 1 - slot)

        @pl.when((i == DATES - 1) & has_raw)
        def _():
            start_lines(far_raw, 1 - slot)

        @pl.when(i < DATES - AHEAD)
        def _():
            edge_start(raw.at[place(i + AHEAD)], i + AHEAD)

        @pl.when((i == DATES - 2) & has_raw)
        def _():
            for copy in raw_copies():
                copy.wait_recv()
            edge_start(far_raw, DATES)

        @pl.when(i < DATES)
        def _():
            for n, of_date in enumerate((line_shift, line_phase, col_shift, col_phase)):
                shifts[n] = of_date[at]

        @pl.when(i >= DATES)
        def _():
            for n, of_date in enumerate((far_shift, far_phase, far_col_shift, far_col_phase)):
                shifts[n] = of_date[at]

        line_off, line_ph, col_off, col_ph = (shifts[n] for n in range(4))
        col_off = col_off - (TAPS // 2 - 1) + 256
        tile_off, rest = col_off // 128, col_off % 128
        line_band = jnp.zeros((ROWS, 2 * SRC), F32)
        band0 = jnp.zeros((256, 256), F32)
        band1 = jnp.zeros((144, 256), F32)
        for k in range(TAPS):
            line_band = jnp.where(line_tap - line_off == k, table[line_ph * TAPS + k], line_band)
            weight = table[col_ph * TAPS + k]
            band0 = jnp.where(col_tap - rest == k, weight, band0)
            band1 = jnp.where(col_tap[:144] + 256 - rest == k, weight, band1)
        line_band = line_band.astype(BF)
        col_band = jnp.concatenate([band0, band1], axis=0).astype(BF)

        for b in range(TILES // 2):
            block = jnp.concatenate(
                [src.at[slot, 2 * b + j].reshape(2 * SRC, 128)[...] for j in range(2)], axis=1
            )
            got = jnp.dot(line_band, block, preferred_element_type=F32).astype(BF)
            azim[2 * b + 2] = got[:, :128]
            azim[2 * b + 3] = got[:, 128:]

        @pl.when(i < count - 1)
        def _():
            edge_wait(i + 1)
            start_edges(i + 1, 1 - slot)

        def ranged(b):
            window = [azim[2 * b + j + tile_off] for j in range(4)]
            window[3] = window[3][:, :16]
            return jnp.dot(
                jnp.concatenate(window, axis=1), col_band, preferred_element_type=F32
            ).astype(BF)

        half_at = [half_place(i, half) for half in range(2)]

        def put(t, value):
            images[half_at[t // HTILES], :, pl.ds((t % HTILES) * 128, 128)] = value

        for b in range(TILES // 2):
            got = ranged(b)
            put(2 * b, got[:, :128])
            put(2 * b + 1, got[:, 128:])
            if 2 * b + 1 == HTILES:
                far_start(i, 0)
        far_start(i, 1)
        pair_copy(i).start()

    def sums(x_at, others):
        count = len(others)

        @pl.loop(0, HTILES)
        def _(c):
            lanes = pl.ds(pl.multiple_of(c * 128, 128), 128)
            x = images[x_at, :, lanes]
            x0, x1 = x[:LINES], x[LINES:]

            def looked_lines(v):
                return (v[:LROWS] + v[LROWS : 2 * LROWS]) + (
                    v[2 * LROWS : 3 * LROWS] + v[3 * LROWS :]
                )

            lhs[pl.ds(0, LROWS), lanes] = looked_lines(x0 * x0 + x1 * x1)
            for n, y_at in enumerate(others):
                y = images[y_at, :, lanes]
                y0, y1 = y[:LINES], y[LINES:]
                row = LROWS * (1 + 2 * n)
                lhs[pl.ds(row, LROWS), lanes] = looked_lines(y0 * x0 + y1 * x1)
                lhs[pl.ds(row + LROWS, LROWS), lanes] = looked_lines(y1 * x0 - y0 * x1)

        total = jnp.dot(
            lhs[pl.ds(0, LROWS * (1 + 2 * count))], look[...], preferred_element_type=F32
        )
        here = total[:LROWS]
        power[x_at] = here
        results = []
        for n, y_at in enumerate(others):
            scale = 1.0 / jnp.sqrt(here * power[y_at] + EPSILON)
            row = LROWS * (1 + 2 * n)
            results.append((total[row : row + LROWS] * scale, total[row + LROWS : row + 2 * LROWS] * scale))
        return results

    def result_copy(u):
        return pltpu.make_async_remote_copy(
            src_ref=mine.at[u],
            dst_ref=theirs.at[u],
            send_sem=res_send.at[u],
            recv_sem=res_recv.at[u],
            device_id=(partner, s),
            device_id_type=MESH,
        )

    def later(u, first_lag, last_lag):
        x_at = OWN0 + u
        lag_list = list(range(first_lag, last_lag + 1))
        results = sums(x_at, [x_at - lag for lag in lag_list])
        for lag, (re_part, im_part) in zip(lag_list, results):
            mine[u - UFIRST, lag - MINLAG, 0] = re_part
            mine[u - UFIRST, lag - MINLAG, 1] = im_part
        result_copy(u - UFIRST).start()

    pass_on(RELAYED[0])

    @pl.loop(0, DATES + partner_raw.astype(jnp.int32))
    def _(i):
        pair_copy(i).wait_recv()

    @pl.loop(0, MINLAG)
    def _(u):
        sums(OWN0 + u, [])

    for u in range(MINLAG, MAXLAG):
        later(u, MINLAG, u)
        if u == PASS_AT:
            pass_on(RELAYED[1])

    @pl.loop(MAXLAG, 2 * DATES)
    def _(u):
        later(u, MINLAG, MAXLAG)

    def back_copy(i):
        return pltpu.make_async_remote_copy(
            src_ref=send_back.at[i, pl.ds(0, MOVED - i)],
            dst_ref=back.at[core, i, pl.ds(0, MOVED - i)],
            send_sem=back_send.at[i],
            recv_sem=back_recv.at[core, i],
            device_id=(2 * chip - 1, s),
            device_id_type=MESH,
        )

    for i in range(MOVED):
        @pl.when(has_prev)
        def _():
            @pl.when((i > 0) | (chip == 4))
            def _():
                far_arrived(1, i).wait_recv()

            results = sums(OWN0 - 1 - i, [OWN0 + u for u in range(MOVED, 2 * MOVED - i)])
            for n, (re_part, im_part) in enumerate(results):
                send_back[i, n, 0] = re_part.astype(BF)
                send_back[i, n, 1] = (-im_part).astype(BF)
            back_copy(i).start()

        @pl.when(has_next)
        def _():
            @pl.when((i > 0) | (chip == 3))
            def _():
                far_arrived(0, i).wait_recv()

            later(2 * DATES + i, max(MINLAG, i + 1), MAXLAG)

    @pl.loop(0, 2 * DATES - UFIRST)
    def _(u):
        result_copy(u).wait_recv()

    @pl.when(has_next)
    def _():
        @pl.loop(2 * DATES - UFIRST, UCOUNT)
        def _(u):
            result_copy(u).wait_recv()

    def back_arrived(half, i):
        return pltpu.make_async_remote_copy(
            src_ref=send_back.at[i, pl.ds(0, MOVED - i)],
            dst_ref=back.at[half, i, pl.ds(0, MOVED - i)],
            send_sem=back_send.at[i], recv_sem=back_recv.at[half, i],
            device_id=(partner, s), device_id_type=MESH,
        )

    @pl.when(has_next & (core == 1))
    def _():
        for i in range(MOVED):
            back_arrived(0, i).wait_recv()
            back_arrived(1, i).wait_recv()

    @pl.loop(0, DATES)
    def _(j):
        t = DATES * core + j
        row = jnp.clip(2 * DATES - 1 - t, 0, MOVED - 1)
        for slot in range(4):
            lag = lags[slot, j]
            u = t + lag
            at = jnp.clip(u - UFIRST, 0, UCOUNT - 1)
            which = jnp.clip(lag - MINLAG, 0, LAGS - 1)
            far_at = jnp.clip(u - 2 * DATES - MOVED, 0, MOVED - 1)
            from_back = u >= 2 * DATES + MOVED
            for part in range(2):
                own, got = mine[at, which, part], theirs[at, which, part]
                left = jnp.where(core == 0, own, got)
                right = jnp.where(core == 0, got, own)
                left = jnp.where(from_back, back[0, row, far_at, part].astype(F32), left)
                right = jnp.where(from_back, back[1, row, far_at, part].astype(F32), right)
                value = jnp.concatenate([left, right], axis=1)
                out[j, slot, part] = jnp.where(lag > 0, value, 0.0)

    @pl.loop(0, count)
    def _(i):
        @pl.when(has_down)
        def _():
            edge_copy(None, i, 0).wait_send()

        @pl.when(has_up)
        def _():
            edge_copy(None, i, 1).wait_send()

        pair_copy(i).wait_send()

    @pl.when(has_raw)
    def _():
        for copy in raw_copies():
            copy.wait_send()

    @pl.when(far_ok)
    def _():
        @pl.loop(jnp.where(crossing, 0, 1), MOVED)
        def _(i):
            far_copy(i, 0).wait_send()
            far_copy(i, 1).wait_send()

    @pl.loop(0, 2 * DATES - UFIRST)
    def _(u):
        result_copy(u).wait_send()

    @pl.when(has_next)
    def _():
        @pl.loop(2 * DATES - UFIRST, UCOUNT)
        def _(u):
            result_copy(u).wait_send()

    @pl.when(has_prev)
    def _():
        for i in range(MOVED):
            back_copy(i).wait_send()

    @pl.when(relaying)
    def _():
        for i in RELAYED:
            relay_out(i).wait_send()


def on_device(raw_slc, line_shift, line_phase, col_shift, col_phase, pair_lags):
    smem = pl.BlockSpec(memory_space=pltpu.SMEM)
    dma = pltpu.SemaphoreType.DMA
    part = (2, LROWS, LOOKS)
    return pl.pallas_call(
        kernel,
        out_shape=jax.ShapeDtypeStruct((DATES, 4, 2, LROWS, 2 * LOOKS), F32),
        in_specs=[pl.BlockSpec(memory_space=pl.ANY)] + [smem] * 6,
        out_specs=pl.BlockSpec(memory_space=pltpu.VMEM),
        scratch_shapes=[
            pltpu.VMEM((IMAGES + DATES + 1, ROWS, HALF), BF),
            pltpu.VMEM((len(RELAYED), ROWS, HALF), BF),
            pltpu.VMEM((DATES + 1, 2, EDGE, 2, COLS), BF),
            pltpu.VMEM((LINES, 2, COLS), BF),
            pltpu.SMEM((DATES,), jnp.int32),
            pltpu.SMEM((DATES,), jnp.int32),
            pltpu.SMEM((DATES,), jnp.int32),
            pltpu.SMEM((DATES,), jnp.int32),
            pltpu.SMEM((4,), jnp.int32),
            pltpu.VMEM((2, TILES, SRC, 2, 128), BF),
            pltpu.VMEM((TILES + 5, ROWS, 128), BF),
            pltpu.VMEM((LROWS * (1 + 2 * LAGS), HALF), BF),
            pltpu.VMEM((HALF, LOOKS), BF),
            pltpu.VMEM((IMAGES, LROWS, LOOKS), F32),
            pltpu.VMEM((UCOUNT, LAGS) + part, F32),
            pltpu.VMEM((UCOUNT, LAGS) + part, F32),
            pltpu.VMEM((2, MOVED, MOVED) + part, BF),
            pltpu.VMEM((MOVED, MOVED) + part, BF),
            dma((2,)),
            dma((DATES + 1, 2)),
            dma((DATES + 1, 2)),
            dma((DATES + 1,)),
            dma((DATES + 1,)),
            dma((MOVED, 2)),
            dma((2, MOVED)),
            dma((UCOUNT,)),
            dma((UCOUNT,)),
            dma((MOVED,)),
            dma((2, MOVED)),
            dma((len(RELAYED),)),
            dma((len(RELAYED),)),
            dma((5,)),
            dma((5,)),
        ],
        compiler_params=pltpu.CompilerParams(
            collective_id=0, has_side_effects=True, vmem_limit_bytes=56 * 1024 * 1024
        ),
        name="coherence_stack",
    )(raw_slc, line_shift, line_phase, col_shift, col_phase, pair_lags.T, jnp.asarray(sinc_table()))


def solution(mesh):
    return jax.shard_map(
        on_device,
        mesh=mesh,
        in_specs=(
            P("date", "strip", None, None),
            P("date"),
            P("date"),
            P("date"),
            P("date"),
            P("date", None),
        ),
        out_specs=P("date", None, None, "strip", None),
        check_vma=False,
    )
```

```python
import functools

import jax
import jax.numpy as jnp
import numpy as np
from jax import lax
from jax.experimental import pallas as pl
from jax.experimental.pallas import tpu as pltpu
from jax.sharding import PartitionSpec as P

TAPS = 8
PHASES = 16
LOOK_A = 4
LOOK_R = 20
MINLAG = 4
MAXLAG = 10
EPSILON = 1e-06

LAGS = MAXLAG - MINLAG + 1
DATES = 8
LINES = 64
COLS = 3840
TILES = COLS // 128
HALF = COLS // 2
HTILES = HALF // 128
LOOKS = HALF // LOOK_R
LROWS = LINES // LOOK_A
ROWS = 2 * LINES
EDGE = TAPS // 2
SRC = LINES + 2 * EDGE
MOVED = 5
OWN0 = MOVED
NEXT0 = OWN0 + 2 * DATES
IMAGES = NEXT0 + MOVED
RELAYED = (0, 1)
RELAYS = ((7, 14, 8), (7, 15, 9), (8, 0, 6), (8, 1, 7))
AHEAD = 4
PASS_AT = 6
CROSSED_ORDER = (2, 3, 0, 4, 1)
OTHER0 = IMAGES
UFIRST = MINLAG
UCOUNT = 2 * DATES + MOVED - UFIRST

BF = jnp.bfloat16
F32 = jnp.float32
MESH = pl.DeviceIdType.MESH


def sinc_table():
    phase = np.arange(PHASES)[:, None] / PHASES
    offset = np.arange(TAPS)[None, :] - (TAPS // 2 - 1) - phase
    weights = np.sinc(offset) * (0.5 + 0.5 * np.cos(np.pi * offset / (TAPS // 2 + 0.5)))
    weights = (weights / weights.sum(axis=1, keepdims=True)).astype(np.float32)
    return weights.astype(BF).astype(np.float32).reshape(-1)


def kernel(
    raw, line_shift, line_phase, col_shift, col_phase, lags, table,
    out,
    images, relay, halo, far_raw, far_shift, far_phase, far_col_shift, far_col_phase, shifts,
    src, azim, lhs, look, power, mine, theirs, back, send_back,
    load_sem, halo_send, halo_recv, pair_send, pair_recv, far_send, far_recv,
    res_send, res_recv, back_send, back_recv, relay_send, relay_recv, raw_send, raw_recv,
):
    d, s = lax.axis_index("date"), lax.axis_index("strip")
    n_date, n_strip = lax.axis_size("date"), lax.axis_size("strip")
    core = d % 2
    chip = d // 2
    has_next = chip < n_date // 2 - 1
    has_prev = chip > 0
    has_up = s > 0
    has_down = s < n_strip - 1
    partner = d + 1 - 2 * core
    far_ok = jnp.where(core == 0, has_prev, has_next)
    far_chip = jnp.where(core == 0, chip - 1, chip + 1)

    crossing = (d == 7) | (d == 8)
    relaying = (d < 2) | (d >= n_date - 2)
    across = (s + n_strip // 2) % n_strip

    def place(i):
        return jnp.where(core == 0, i, DATES - 1 - i)

    far_device = jnp.where(core == 0, d - 1, d + 1)
    far_image = jnp.where(core == 0, OWN0 - 1, NEXT0)
    has_raw = far_ok & jnp.logical_not(crossing)
    partner_raw = jnp.where(core == 0, has_next & (chip != 3), has_prev & (chip != 4))

    def raw_copies():
        pairs = (
            (raw.at[place(0)], far_raw),
            (line_shift, far_shift),
            (line_phase, far_phase),
            (col_shift, far_col_shift),
            (col_phase, far_col_phase),
        )
        return [
            pltpu.make_async_remote_copy(
                src_ref=a, dst_ref=b, send_sem=raw_send.at[n], recv_sem=raw_recv.at[n],
                device_id=(far_device, s), device_id_type=MESH,
            )
            for n, (a, b) in enumerate(pairs)
        ]

    def load_tile(lines, slot, c):
        return pltpu.make_async_copy(
            lines.at[:, :, pl.ds(pl.multiple_of(c * 128, 128), 128)],
            src.at[slot, c, pl.ds(EDGE, LINES)],
            load_sem.at[slot],
        )

    def load_edges(i, slot, c, side):
        return pltpu.make_async_copy(
            halo.at[i, side, :, :, pl.ds(pl.multiple_of(c * 128, 128), 128)],
            src.at[slot, c, pl.ds(side * (EDGE + LINES), EDGE)],
            load_sem.at[slot],
        )

    def start_lines(lines, slot):
        @pl.loop(0, TILES)
        def _(c):
            load_tile(lines, slot, c).start()

    def start_edges(i, slot):
        @pl.loop(0, TILES)
        def _(c):
            load_edges(i, slot, c, 0).start()
            load_edges(i, slot, c, 1).start()

    start_lines(raw.at[place(0)], 0)

    barrier = pltpu.get_barrier_semaphore()
    peers = 0
    for step in (-2, -1, 1, 2):
        ok = (d + step >= 0) & (d + step < n_date)
        peers = peers + ok.astype(jnp.int32)

        @pl.when(ok)
        def _():
            pl.semaphore_signal(barrier, inc=1, device_id=(d + step, s), device_id_type=MESH)

    for step, ok in ((-1, has_up), (1, has_down)):
        peers = peers + ok.astype(jnp.int32)

        @pl.when(ok)
        def _():
            pl.semaphore_signal(barrier, inc=1, device_id=(d, s + step), device_id_type=MESH)

    for a, b in sorted({(min(p), max(p)) for x, y, z in RELAYS for p in ((x, y), (y, z))}):
        for here, there in ((a, b), (b, a)):
            peers = peers + (d == here).astype(jnp.int32)

            @pl.when(d == here)
            def _():
                pl.semaphore_signal(barrier, inc=1, device_id=(there, across), device_id_type=MESH)

    pl.semaphore_wait(barrier, peers)

    def edge_copy(lines, i, side):
        return pltpu.make_async_remote_copy(
            src_ref=halo.at[i, side] if lines is None else lines.at[
                pl.ds((1 - side) * (LINES - EDGE), EDGE)
            ],
            dst_ref=halo.at[i, side],
            send_sem=halo_send.at[i, side],
            recv_sem=halo_recv.at[i, side],
            device_id=(d, s + 1 - 2 * side),
            device_id_type=MESH,
        )

    def edge_start(lines, i):
        @pl.when(has_down)
        def _():
            edge_copy(lines, i, 0).start()

        @pl.when(has_up)
        def _():
            edge_copy(lines, i, 1).start()

    edge_start(raw.at[place(0)], 0)

    @pl.when(has_raw)
    def _():
        for copy in raw_copies():
            copy.start()

    @pl.when(jnp.logical_not(has_up))
    def _():
        @pl.loop(0, DATES + 1)
        def _(i):
            halo[i, 0] = jnp.zeros((EDGE, 2, COLS), BF)

    @pl.when(jnp.logical_not(has_down))
    def _():
        @pl.loop(0, DATES + 1)
        def _(i):
            halo[i, 1] = jnp.zeros((EDGE, 2, COLS), BF)

    for t in (0, 1, TILES + 2, TILES + 3, TILES + 4):
        azim[t] = jnp.zeros((ROWS, 128), BF)
    look_row = lax.broadcasted_iota(jnp.int32, (HALF, LOOKS), 0)
    look_col = lax.broadcasted_iota(jnp.int32, (HALF, LOOKS), 1) * LOOK_R
    look[...] = jnp.where(
        (look_row >= look_col) & (look_row < look_col + LOOK_R), 1.0, 0.0
    ).astype(BF)

    def edge_wait(i):
        @pl.when(has_up)
        def _():
            edge_copy(None, i, 0).wait_recv()

        @pl.when(has_down)
        def _():
            edge_copy(None, i, 1).wait_recv()

    def own_place(i):
        return jnp.where(i < DATES, OWN0 + DATES * core + place(i), far_image)

    def half_place(i, half):
        return jnp.where(core == half, own_place(i), OTHER0 + i)

    def far_copy(i, half):
        return pltpu.make_async_remote_copy(
            src_ref=images.at[half_place(i, half)],
            dst_ref=images.at[jnp.where(core == 0, NEXT0 + i, OWN0 - 1 - i)],
            send_sem=far_send.at[i, half],
            recv_sem=far_recv.at[core, i],
            device_id=(2 * far_chip + half, s),
            device_id_type=MESH,
        )

    def relay_in(i, half):
        return pltpu.make_async_remote_copy(
            src_ref=images.at[half_place(i, half)],
            dst_ref=relay.at[i - RELAYED[0]],
            send_sem=far_send.at[i, half],
            recv_sem=relay_recv.at[i - RELAYED[0]],
            device_id=(jnp.where(d == 7, n_date - 2, 0) + half, across),
            device_id_type=MESH,
        )

    def relay_out(i):
        return pltpu.make_async_remote_copy(
            src_ref=relay.at[i - RELAYED[0]],
            dst_ref=images.at[jnp.where(d < 2, NEXT0 + i, OWN0 - 1 - i)],
            send_sem=relay_send.at[i - RELAYED[0]],
            recv_sem=far_recv.at[jnp.where(d < 2, 0, 1), i],
            device_id=(jnp.where(d < 2, d + 6, d - 6), across),
            device_id_type=MESH,
        )

    def pass_on(i):
        @pl.when(relaying)
        def _():
            relay_in(i, 0).wait_recv()
            relay_out(i).start()

    def far_start(i, half):
        relayed = crossing & (i >= RELAYED[0]) & (i <= RELAYED[-1])

        direct = far_ok & (i < MOVED) & ((i > 0) | crossing) & jnp.logical_not(relayed)

        @pl.when(direct)
        def _():
            far_copy(i, half).start()

        @pl.when(relayed)
        def _():
            relay_in(i, half).start()

    def far_arrived(side, i):
        at = NEXT0 + i if side == 0 else OWN0 - 1 - i
        return pltpu.make_async_remote_copy(
            src_ref=images.at[at], dst_ref=images.at[at],
            send_sem=far_send.at[i, 0], recv_sem=far_recv.at[side, i],
            device_id=(partner, s), device_id_type=MESH,
        )

    def pair_copy(i):
        return pltpu.make_async_remote_copy(
            src_ref=images.at[OTHER0 + i],
            dst_ref=images.at[own_place(i)],
            send_sem=pair_send.at[i],
            recv_sem=pair_recv.at[i],
            device_id=(partner, s),
            device_id_type=MESH,
        )

    out_row = lax.broadcasted_iota(jnp.int32, (ROWS, 2 * SRC), 0)
    src_row = lax.broadcasted_iota(jnp.int32, (ROWS, 2 * SRC), 1)
    within = out_row % LINES
    out_line = (within % LROWS) * LOOK_A + within // LROWS
    line_tap = jnp.where(src_row % 2 == out_row // LINES, src_row // 2 - out_line - 1, 1000)
    col_tap = lax.broadcasted_iota(jnp.int32, (256, 256), 0) - lax.broadcasted_iota(
        jnp.int32, (256, 256), 1
    )

    for n in range(1, AHEAD):
        edge_start(raw.at[place(n)], n)
    edge_wait(0)
    start_edges(0, 0)

    count = DATES + has_raw.astype(jnp.int32)

    @pl.loop(0, count)
    def _(i):
        slot = i % 2
        at = jnp.where(i < DATES, place(i), jnp.where(core == 0, DATES - 1, 0))
        pltpu.make_async_copy(
            src.at[slot], src.at[slot], load_sem.at[slot]
        ).wait()

        @pl.when(i < DATES - 1)
        def _():
            start_lines(raw.at[place(i + 1)], 1 - slot)

        @pl.when((i == DATES - 1) & has_raw)
        def _():
            start_lines(far_raw, 1 - slot)

        @pl.when(i < DATES - AHEAD)
        def _():
            edge_start(raw.at[place(i + AHEAD)], i + AHEAD)

        @pl.when((i == DATES - 2) & has_raw)
        def _():
            for copy in raw_copies():
                copy.wait_recv()
            edge_start(far_raw, DATES)

        @pl.when(i < DATES)
        def _():
            for n, of_date in enumerate((line_shift, line_phase, col_shift, col_phase)):
                shifts[n] = of_date[at]

        @pl.when(i >= DATES)
        def _():
            for n, of_date in enumerate((far_shift, far_phase, far_col_shift, far_col_phase)):
                shifts[n] = of_date[at]

        line_off, line_ph, col_off, col_ph = (shifts[n] for n in range(4))
        col_off = col_off - (TAPS // 2 - 1) + 256
        tile_off, rest = col_off // 128, col_off % 128
        line_band = jnp.zeros((ROWS, 2 * SRC), F32)
        band0 = jnp.zeros((256, 256), F32)
        band1 = jnp.zeros((144, 256), F32)
        for k in range(TAPS):
            line_band = jnp.where(line_tap - line_off == k, table[line_ph * TAPS + k], line_band)
            weight = table[col_ph * TAPS + k]
            band0 = jnp.where(col_tap - rest == k, weight, band0)
            band1 = jnp.where(col_tap[:144] + 256 - rest == k, weight, band1)
        line_band = line_band.astype(BF)
        col_band = jnp.concatenate([band0, band1], axis=0).astype(BF)

        for b in range(TILES // 2):
            block = jnp.concatenate(
                [src.at[slot, 2 * b + j].reshape(2 * SRC, 128)[...] for j in range(2)], axis=1
            )
            got = jnp.dot(line_band, block, preferred_element_type=F32).astype(BF)
            azim[2 * b + 2] = got[:, :128]
            azim[2 * b + 3] = got[:, 128:]

        @pl.when(i < count - 1)
        def _():
            edge_wait(i + 1)
            start_edges(i + 1, 1 - slot)

        def ranged(b):
            window = [azim[2 * b + j + tile_off] for j in range(4)]
            window[3] = window[3][:, :16]
            return jnp.dot(
                jnp.concatenate(window, axis=1), col_band, preferred_element_type=F32
            ).astype(BF)

        half_at = [half_place(i, half) for half in range(2)]

        def put(t, value):
            images[half_at[t // HTILES], :, pl.ds((t % HTILES) * 128, 128)] = value

        for b in range(TILES // 2):
            got = ranged(b)
            put(2 * b, got[:, :128])
            put(2 * b + 1, got[:, 128:])
            if 2 * b + 1 == HTILES:
                far_start(i, 0)
        far_start(i, 1)
        pair_copy(i).start()

    def sums(x_at, others):
        count = len(others)

        @pl.loop(0, HTILES)
        def _(c):
            lanes = pl.ds(pl.multiple_of(c * 128, 128), 128)
            x = images[x_at, :, lanes]
            x0, x1 = x[:LINES], x[LINES:]

            def looked_lines(v):
                return (v[:LROWS] + v[LROWS : 2 * LROWS]) + (
                    v[2 * LROWS : 3 * LROWS] + v[3 * LROWS :]
                )

            lhs[pl.ds(0, LROWS), lanes] = looked_lines(x0 * x0 + x1 * x1)
            for n, y_at in enumerate(others):
                y = images[y_at, :, lanes]
                y0, y1 = y[:LINES], y[LINES:]
                row = LROWS * (1 + 2 * n)
                lhs[pl.ds(row, LROWS), lanes] = looked_lines(y0 * x0 + y1 * x1)
                lhs[pl.ds(row + LROWS, LROWS), lanes] = looked_lines(y1 * x0 - y0 * x1)

        total = jnp.dot(
            lhs[pl.ds(0, LROWS * (1 + 2 * count))], look[...], preferred_element_type=F32
        )
        here = total[:LROWS]
        power[x_at] = here
        results = []
        for n, y_at in enumerate(others):
            scale = 1.0 / jnp.sqrt(here * power[y_at] + EPSILON)
            row = LROWS * (1 + 2 * n)
            results.append((total[row : row + LROWS] * scale, total[row + LROWS : row + 2 * LROWS] * scale))
        return results

    def result_copy(u):
        return pltpu.make_async_remote_copy(
            src_ref=mine.at[u],
            dst_ref=theirs.at[u],
            send_sem=res_send.at[u],
            recv_sem=res_recv.at[u],
            device_id=(partner, s),
            device_id_type=MESH,
        )

    def later(u, first_lag, last_lag):
        x_at = OWN0 + u
        lag_list = list(range(first_lag, last_lag + 1))
        results = sums(x_at, [x_at - lag for lag in lag_list])
        for lag, (re_part, im_part) in zip(lag_list, results):
            mine[u - UFIRST, lag - MINLAG, 0] = re_part
            mine[u - UFIRST, lag - MINLAG, 1] = im_part
        result_copy(u - UFIRST).start()

    pass_on(RELAYED[0])

    def pairs_arrived(first, end):
        @pl.loop(first, end)
        def _(i):
            pair_copy(i).wait_recv()

    pairs_arrived(0, MINLAG)

    @pl.loop(0, MINLAG)
    def _(u):
        sums(OWN0 + u, [])

    pairs_arrived(MINLAG, DATES - 1)
    for u in range(MINLAG, MAXLAG):
        if u == DATES - 1:
            pairs_arrived(DATES - 1, DATES)
        later(u, MINLAG, u)
        if u == PASS_AT:
            pass_on(RELAYED[1])

    @pl.loop(MAXLAG, 2 * DATES)
    def _(u):
        later(u, MINLAG, MAXLAG)

    @pl.when(partner_raw)
    def _():
        pair_copy(DATES).wait_recv()

    def back_copy(i):
        return pltpu.make_async_remote_copy(
            src_ref=send_back.at[i, pl.ds(0, MOVED - i)],
            dst_ref=back.at[core, i, pl.ds(0, MOVED - i)],
            send_sem=back_send.at[i],
            recv_sem=back_recv.at[core, i],
            device_id=(2 * chip - 1, s),
            device_id_type=MESH,
        )

    def from_next(i, sent):
        if sent:
            far_arrived(0, i).wait_recv()
        later(2 * DATES + i, max(MINLAG, i + 1), MAXLAG)

    def from_prev(i, sent):
        if sent:
            far_arrived(1, i).wait_recv()
        results = sums(OWN0 - 1 - i, [OWN0 + u for u in range(MOVED, 2 * MOVED - i)])
        for n, (re_part, im_part) in enumerate(results):
            send_back[i, n, 0] = re_part.astype(BF)
            send_back[i, n, 1] = (-im_part).astype(BF)
        back_copy(i).start()

    for i, crossed in enumerate(CROSSED_ORDER):
        pl.when(has_prev & (chip != 4))(functools.partial(from_prev, i, i > 0))
        pl.when(chip == 4)(functools.partial(from_prev, crossed, True))
        pl.when(has_next & (chip != 3))(functools.partial(from_next, i, i > 0))
        pl.when(chip == 3)(functools.partial(from_next, crossed, True))

    @pl.loop(0, 2 * DATES - UFIRST)
    def _(u):
        result_copy(u).wait_recv()

    @pl.when(has_next)
    def _():
        @pl.loop(2 * DATES - UFIRST, UCOUNT)
        def _(u):
            result_copy(u).wait_recv()

    def back_arrived(half, i):
        return pltpu.make_async_remote_copy(
            src_ref=send_back.at[i, pl.ds(0, MOVED - i)],
            dst_ref=back.at[half, i, pl.ds(0, MOVED - i)],
            send_sem=back_send.at[i], recv_sem=back_recv.at[half, i],
            device_id=(partner, s), device_id_type=MESH,
        )

    @pl.when(has_next & (core == 1))
    def _():
        for i in range(MOVED):
            back_arrived(0, i).wait_recv()
            back_arrived(1, i).wait_recv()

    @pl.loop(0, DATES)
    def _(j):
        t = DATES * core + j
        row = jnp.clip(2 * DATES - 1 - t, 0, MOVED - 1)
        for slot in range(4):
            lag = lags[slot, j]
            u = t + lag
            at = jnp.clip(u - UFIRST, 0, UCOUNT - 1)
            which = jnp.clip(lag - MINLAG, 0, LAGS - 1)
            far_at = jnp.clip(u - 2 * DATES - MOVED, 0, MOVED - 1)
            from_back = u >= 2 * DATES + MOVED
            for part in range(2):
                own, got = mine[at, which, part], theirs[at, which, part]
                left = jnp.where(core == 0, own, got)
                right = jnp.where(core == 0, got, own)
                left = jnp.where(from_back, back[0, row, far_at, part].astype(F32), left)
                right = jnp.where(from_back, back[1, row, far_at, part].astype(F32), right)
                value = jnp.concatenate([left, right], axis=1)
                out[j, slot, part] = jnp.where(lag > 0, value, 0.0)

    @pl.loop(0, count)
    def _(i):
        @pl.when(has_down)
        def _():
            edge_copy(None, i, 0).wait_send()

        @pl.when(has_up)
        def _():
            edge_copy(None, i, 1).wait_send()

        pair_copy(i).wait_send()

    @pl.when(has_raw)
    def _():
        for copy in raw_copies():
            copy.wait_send()

    @pl.when(far_ok)
    def _():
        @pl.loop(jnp.where(crossing, 0, 1), MOVED)
        def _(i):
            far_copy(i, 0).wait_send()
            far_copy(i, 1).wait_send()

    @pl.loop(0, 2 * DATES - UFIRST)
    def _(u):
        result_copy(u).wait_send()

    @pl.when(has_next)
    def _():
        @pl.loop(2 * DATES - UFIRST, UCOUNT)
        def _(u):
            result_copy(u).wait_send()

    @pl.when(has_prev)
    def _():
        for i in range(MOVED):
            back_copy(i).wait_send()

    @pl.when(relaying)
    def _():
        for i in RELAYED:
            relay_out(i).wait_send()


def on_device(raw_slc, line_shift, line_phase, col_shift, col_phase, pair_lags):
    smem = pl.BlockSpec(memory_space=pltpu.SMEM)
    dma = pltpu.SemaphoreType.DMA
    part = (2, LROWS, LOOKS)
    return pl.pallas_call(
        kernel,
        out_shape=jax.ShapeDtypeStruct((DATES, 4, 2, LROWS, 2 * LOOKS), F32),
        in_specs=[pl.BlockSpec(memory_space=pl.ANY)] + [smem] * 6,
        out_specs=pl.BlockSpec(memory_space=pltpu.VMEM),
        scratch_shapes=[
            pltpu.VMEM((IMAGES + DATES + 1, ROWS, HALF), BF),
            pltpu.VMEM((len(RELAYED), ROWS, HALF), BF),
            pltpu.VMEM((DATES + 1, 2, EDGE, 2, COLS), BF),
            pltpu.VMEM((LINES, 2, COLS), BF),
            pltpu.SMEM((DATES,), jnp.int32),
            pltpu.SMEM((DATES,), jnp.int32),
            pltpu.SMEM((DATES,), jnp.int32),
            pltpu.SMEM((DATES,), jnp.int32),
            pltpu.SMEM((4,), jnp.int32),
            pltpu.VMEM((2, TILES, SRC, 2, 128), BF),
            pltpu.VMEM((TILES + 5, ROWS, 128), BF),
            pltpu.VMEM((LROWS * (1 + 2 * LAGS), HALF), BF),
            pltpu.VMEM((HALF, LOOKS), BF),
            pltpu.VMEM((IMAGES, LROWS, LOOKS), F32),
            pltpu.VMEM((UCOUNT, LAGS) + part, F32),
            pltpu.VMEM((UCOUNT, LAGS) + part, F32),
            pltpu.VMEM((2, MOVED, MOVED) + part, BF),
            pltpu.VMEM((MOVED, MOVED) + part, BF),
            dma((2,)),
            dma((DATES + 1, 2)),
            dma((DATES + 1, 2)),
            dma((DATES + 1,)),
            dma((DATES + 1,)),
            dma((MOVED, 2)),
            dma((2, MOVED)),
            dma((UCOUNT,)),
            dma((UCOUNT,)),
            dma((MOVED,)),
            dma((2, MOVED)),
            dma((len(RELAYED),)),
            dma((len(RELAYED),)),
            dma((5,)),
            dma((5,)),
        ],
        compiler_params=pltpu.CompilerParams(
            collective_id=0, has_side_effects=True, vmem_limit_bytes=56 * 1024 * 1024
        ),
        name="coherence_stack",
    )(raw_slc, line_shift, line_phase, col_shift, col_phase, pair_lags.T, jnp.asarray(sinc_table()))


def solution(mesh):
    return jax.shard_map(
        on_device,
        mesh=mesh,
        in_specs=(
            P("date", "strip", None, None),
            P("date"),
            P("date"),
            P("date"),
            P("date"),
            P("date", None),
        ),
        out_specs=P("date", None, None, "strip", None),
        check_vma=False,
    )
```

```python
import functools

import jax
import jax.numpy as jnp
import numpy as np
from jax import lax
from jax.experimental import pallas as pl
from jax.experimental.pallas import tpu as pltpu
from jax.sharding import PartitionSpec as P

TAPS = 8
PHASES = 16
LOOK_A = 4
LOOK_R = 20
MINLAG = 4
MAXLAG = 10
EPSILON = 1e-06

LAGS = MAXLAG - MINLAG + 1
DATES = 8
LINES = 64
COLS = 3840
TILES = COLS // 128
HALF = COLS // 2
HTILES = HALF // 128
LOOKS = HALF // LOOK_R
LROWS = LINES // LOOK_A
ROWS = 2 * LINES
EDGE = TAPS // 2
SRC = LINES + 2 * EDGE
MOVED = 5
OWN0 = MOVED
NEXT0 = OWN0 + 2 * DATES
IMAGES = NEXT0 + MOVED
RELAYED = (0, 1)
RELAYS = ((7, 14, 8), (7, 15, 9), (8, 0, 6), (8, 1, 7))
AHEAD = 4
PASS_AT = 6
CROSSED_ORDER = (2, 3, 0, 4, 1)
OTHER0 = IMAGES
UFIRST = MINLAG
UCOUNT = 2 * DATES + MOVED - UFIRST

BF = jnp.bfloat16
F32 = jnp.float32
MESH = pl.DeviceIdType.MESH


def sinc_table():
    phase = np.arange(PHASES)[:, None] / PHASES
    offset = np.arange(TAPS)[None, :] - (TAPS // 2 - 1) - phase
    weights = np.sinc(offset) * (0.5 + 0.5 * np.cos(np.pi * offset / (TAPS // 2 + 0.5)))
    weights = (weights / weights.sum(axis=1, keepdims=True)).astype(np.float32)
    return weights.astype(BF).astype(np.float32).reshape(-1)


def kernel(
    raw, line_shift, line_phase, col_shift, col_phase, lags, table,
    out,
    images, relay, halo, far_raw, far_shift, far_phase, far_col_shift, far_col_phase, shifts,
    src, azim, lhs, look, power, mine, theirs, back, send_back,
    load_sem, halo_send, halo_recv, pair_send, pair_recv, far_send, far_recv,
    res_send, res_recv, back_send, back_recv, relay_send, relay_recv, raw_send, raw_recv,
):
    d, s = lax.axis_index("date"), lax.axis_index("strip")
    n_date, n_strip = lax.axis_size("date"), lax.axis_size("strip")
    core = d % 2
    chip = d // 2
    has_next = chip < n_date // 2 - 1
    has_prev = chip > 0
    has_up = s > 0
    has_down = s < n_strip - 1
    partner = d + 1 - 2 * core
    far_ok = jnp.where(core == 0, has_prev, has_next)
    far_chip = jnp.where(core == 0, chip - 1, chip + 1)

    crossing = (d == 7) | (d == 8)
    relaying = (d < 2) | (d >= n_date - 2)
    across = (s + n_strip // 2) % n_strip

    def place(i):
        return jnp.where(core == 0, i, DATES - 1 - i)

    far_device = jnp.where(core == 0, d - 1, d + 1)
    far_image = jnp.where(core == 0, OWN0 - 1, NEXT0)
    has_raw = far_ok & jnp.logical_not(crossing)
    partner_raw = jnp.where(core == 0, has_next & (chip != 3), has_prev & (chip != 4))

    def raw_copies():
        pairs = (
            (raw.at[place(0)], far_raw),
            (line_shift, far_shift),
            (line_phase, far_phase),
            (col_shift, far_col_shift),
            (col_phase, far_col_phase),
        )
        return [
            pltpu.make_async_remote_copy(
                src_ref=a, dst_ref=b, send_sem=raw_send.at[n], recv_sem=raw_recv.at[n],
                device_id=(far_device, s), device_id_type=MESH,
            )
            for n, (a, b) in enumerate(pairs)
        ]

    def load_tile(lines, slot, c):
        return pltpu.make_async_copy(
            lines.at[:, :, pl.ds(pl.multiple_of(c * 128, 128), 128)],
            src.at[slot, c, pl.ds(EDGE, LINES)],
            load_sem.at[slot],
        )

    def load_edges(i, slot, c, side):
        return pltpu.make_async_copy(
            halo.at[i, side, :, :, pl.ds(pl.multiple_of(c * 128, 128), 128)],
            src.at[slot, c, pl.ds(side * (EDGE + LINES), EDGE)],
            load_sem.at[slot],
        )

    def start_lines(lines, slot):
        @pl.loop(0, TILES)
        def _(c):
            load_tile(lines, slot, c).start()

    def start_edges(i, slot):
        @pl.loop(0, TILES)
        def _(c):
            load_edges(i, slot, c, 0).start()
            load_edges(i, slot, c, 1).start()

    start_lines(raw.at[place(0)], 0)

    barrier = pltpu.get_barrier_semaphore()
    peers = 0
    for step in (-2, -1, 1, 2):
        ok = (d + step >= 0) & (d + step < n_date)
        peers = peers + ok.astype(jnp.int32)

        @pl.when(ok)
        def _():
            pl.semaphore_signal(barrier, inc=1, device_id=(d + step, s), device_id_type=MESH)

    for step, ok in ((-1, has_up), (1, has_down)):
        peers = peers + ok.astype(jnp.int32)

        @pl.when(ok)
        def _():
            pl.semaphore_signal(barrier, inc=1, device_id=(d, s + step), device_id_type=MESH)

    for a, b in sorted({(min(p), max(p)) for x, y, z in RELAYS for p in ((x, y), (y, z))}):
        for here, there in ((a, b), (b, a)):
            peers = peers + (d == here).astype(jnp.int32)

            @pl.when(d == here)
            def _():
                pl.semaphore_signal(barrier, inc=1, device_id=(there, across), device_id_type=MESH)

    pl.semaphore_wait(barrier, peers)

    def edge_copy(lines, i, side):
        return pltpu.make_async_remote_copy(
            src_ref=halo.at[i, side] if lines is None else lines.at[
                pl.ds((1 - side) * (LINES - EDGE), EDGE)
            ],
            dst_ref=halo.at[i, side],
            send_sem=halo_send.at[i, side],
            recv_sem=halo_recv.at[i, side],
            device_id=(d, s + 1 - 2 * side),
            device_id_type=MESH,
        )

    def edge_start(lines, i):
        @pl.when(has_down)
        def _():
            edge_copy(lines, i, 0).start()

        @pl.when(has_up)
        def _():
            edge_copy(lines, i, 1).start()

    edge_start(raw.at[place(0)], 0)

    @pl.when(has_raw)
    def _():
        for copy in raw_copies():
            copy.start()

    @pl.when(jnp.logical_not(has_up))
    def _():
        @pl.loop(0, DATES + 1)
        def _(i):
            halo[i, 0] = jnp.zeros((EDGE, 2, COLS), BF)

    @pl.when(jnp.logical_not(has_down))
    def _():
        @pl.loop(0, DATES + 1)
        def _(i):
            halo[i, 1] = jnp.zeros((EDGE, 2, COLS), BF)

    for t in (0, 1, TILES + 2, TILES + 3, TILES + 4):
        azim[t] = jnp.zeros((ROWS, 128), BF)
    look_row = lax.broadcasted_iota(jnp.int32, (HALF, LOOKS), 0)
    look_col = lax.broadcasted_iota(jnp.int32, (HALF, LOOKS), 1) * LOOK_R
    look[...] = jnp.where(
        (look_row >= look_col) & (look_row < look_col + LOOK_R), 1.0, 0.0
    ).astype(BF)

    def edge_wait(i):
        @pl.when(has_up)
        def _():
            edge_copy(None, i, 0).wait_recv()

        @pl.when(has_down)
        def _():
            edge_copy(None, i, 1).wait_recv()

    def own_place(i):
        return jnp.where(i < DATES, OWN0 + DATES * core + place(i), far_image)

    def half_place(i, half):
        return jnp.where(core == half, own_place(i), OTHER0 + i)

    def far_copy(i, half):
        return pltpu.make_async_remote_copy(
            src_ref=images.at[half_place(i, half)],
            dst_ref=images.at[jnp.where(core == 0, NEXT0 + i, OWN0 - 1 - i)],
            send_sem=far_send.at[i, half],
            recv_sem=far_recv.at[core, i],
            device_id=(2 * far_chip + half, s),
            device_id_type=MESH,
        )

    def relay_in(i, half):
        return pltpu.make_async_remote_copy(
            src_ref=images.at[half_place(i, half)],
            dst_ref=relay.at[i - RELAYED[0]],
            send_sem=far_send.at[i, half],
            recv_sem=relay_recv.at[i - RELAYED[0]],
            device_id=(jnp.where(d == 7, n_date - 2, 0) + half, across),
            device_id_type=MESH,
        )

    def relay_out(i):
        return pltpu.make_async_remote_copy(
            src_ref=relay.at[i - RELAYED[0]],
            dst_ref=images.at[jnp.where(d < 2, NEXT0 + i, OWN0 - 1 - i)],
            send_sem=relay_send.at[i - RELAYED[0]],
            recv_sem=far_recv.at[jnp.where(d < 2, 0, 1), i],
            device_id=(jnp.where(d < 2, d + 6, d - 6), across),
            device_id_type=MESH,
        )

    def pass_on(i):
        @pl.when(relaying)
        def _():
            relay_in(i, 0).wait_recv()
            relay_out(i).start()

    def far_start(i, half):
        relayed = crossing & (i >= RELAYED[0]) & (i <= RELAYED[-1])

        direct = far_ok & (i < MOVED) & ((i > 0) | crossing) & jnp.logical_not(relayed)

        @pl.when(direct)
        def _():
            far_copy(i, half).start()

        @pl.when(relayed)
        def _():
            relay_in(i, half).start()

    def far_arrived(side, i):
        at = NEXT0 + i if side == 0 else OWN0 - 1 - i
        return pltpu.make_async_remote_copy(
            src_ref=images.at[at], dst_ref=images.at[at],
            send_sem=far_send.at[i, 0], recv_sem=far_recv.at[side, i],
            device_id=(partner, s), device_id_type=MESH,
        )

    def pair_copy(i):
        return pltpu.make_async_remote_copy(
            src_ref=images.at[OTHER0 + i],
            dst_ref=images.at[own_place(i)],
            send_sem=pair_send.at[i],
            recv_sem=pair_recv.at[i],
            device_id=(partner, s),
            device_id_type=MESH,
        )

    out_row = lax.broadcasted_iota(jnp.int32, (ROWS, 2 * SRC), 0)
    src_row = lax.broadcasted_iota(jnp.int32, (ROWS, 2 * SRC), 1)
    within = out_row % LINES
    out_line = (within % LROWS) * LOOK_A + within // LROWS
    line_tap = jnp.where(src_row % 2 == out_row // LINES, src_row // 2 - out_line - 1, 1000)
    col_tap = lax.broadcasted_iota(jnp.int32, (256, 256), 0) - lax.broadcasted_iota(
        jnp.int32, (256, 256), 1
    )

    for n in range(1, AHEAD):
        edge_start(raw.at[place(n)], n)
    edge_wait(0)
    start_edges(0, 0)

    count = DATES + has_raw.astype(jnp.int32)

    @pl.loop(0, count)
    def _(i):
        slot = i % 2
        at = jnp.where(i < DATES, place(i), jnp.where(core == 0, DATES - 1, 0))
        pltpu.make_async_copy(
            src.at[slot], src.at[slot], load_sem.at[slot]
        ).wait()

        @pl.when(i < DATES - 1)
        def _():
            start_lines(raw.at[place(i + 1)], 1 - slot)

        @pl.when((i == DATES - 1) & has_raw)
        def _():
            start_lines(far_raw, 1 - slot)

        @pl.when(i < DATES - AHEAD)
        def _():
            edge_start(raw.at[place(i + AHEAD)], i + AHEAD)

        @pl.when((i == DATES - 2) & has_raw)
        def _():
            for copy in raw_copies():
                copy.wait_recv()
            edge_start(far_raw, DATES)

        @pl.when(i < DATES)
        def _():
            for n, of_date in enumerate((line_shift, line_phase, col_shift, col_phase)):
                shifts[n] = of_date[at]

        @pl.when(i >= DATES)
        def _():
            for n, of_date in enumerate((far_shift, far_phase, far_col_shift, far_col_phase)):
                shifts[n] = of_date[at]

        line_off, line_ph, col_off, col_ph = (shifts[n] for n in range(4))
        col_off = col_off - (TAPS // 2 - 1) + 256
        tile_off, rest = col_off // 128, col_off % 128
        line_band = jnp.zeros((ROWS, 2 * SRC), F32)
        band0 = jnp.zeros((256, 256), F32)
        band1 = jnp.zeros((144, 256), F32)
        for k in range(TAPS):
            line_band = jnp.where(line_tap - line_off == k, table[line_ph * TAPS + k], line_band)
            weight = table[col_ph * TAPS + k]
            band0 = jnp.where(col_tap - rest == k, weight, band0)
            band1 = jnp.where(col_tap[:144] + 256 - rest == k, weight, band1)
        line_band = line_band.astype(BF)
        col_band = jnp.concatenate([band0, band1], axis=0).astype(BF)

        for b in range(TILES // 2):
            block = jnp.concatenate(
                [src.at[slot, 2 * b + j].reshape(2 * SRC, 128)[...] for j in range(2)], axis=1
            )
            got = jnp.dot(line_band, block, preferred_element_type=F32).astype(BF)
            azim[2 * b + 2] = got[:, :128]
            azim[2 * b + 3] = got[:, 128:]

        @pl.when(i < count - 1)
        def _():
            edge_wait(i + 1)
            start_edges(i + 1, 1 - slot)

        def ranged(b):
            window = [azim[2 * b + j + tile_off] for j in range(4)]
            window[3] = window[3][:, :16]
            return jnp.dot(
                jnp.concatenate(window, axis=1), col_band, preferred_element_type=F32
            ).astype(BF)

        half_at = [half_place(i, half) for half in range(2)]

        def put(t, value):
            images[half_at[t // HTILES], :, pl.ds((t % HTILES) * 128, 128)] = value

        for b in range(TILES // 2):
            got = ranged(b)
            put(2 * b, got[:, :128])
            put(2 * b + 1, got[:, 128:])
            if 2 * b + 1 == HTILES:
                far_start(i, 0)
        far_start(i, 1)
        pair_copy(i).start()

    def sums(x_at, others):
        count = len(others)

        @pl.loop(0, HTILES, unroll=5)
        def _(c):
            lanes = pl.ds(pl.multiple_of(c * 128, 128), 128)
            x = images[x_at, :, lanes]
            x0, x1 = x[:LINES], x[LINES:]

            def looked_lines(v):
                return (v[:LROWS] + v[LROWS : 2 * LROWS]) + (
                    v[2 * LROWS : 3 * LROWS] + v[3 * LROWS :]
                )

            lhs[pl.ds(0, LROWS), lanes] = looked_lines(x0 * x0 + x1 * x1)
            for n, y_at in enumerate(others):
                y = images[y_at, :, lanes]
                y0, y1 = y[:LINES], y[LINES:]
                row = LROWS * (1 + 2 * n)
                lhs[pl.ds(row, LROWS), lanes] = looked_lines(y0 * x0 + y1 * x1)
                lhs[pl.ds(row + LROWS, LROWS), lanes] = looked_lines(y1 * x0 - y0 * x1)

        total = jnp.dot(
            lhs[pl.ds(0, LROWS * (1 + 2 * count))], look[...], preferred_element_type=F32
        )
        here = total[:LROWS]
        power[x_at] = here
        results = []
        for n, y_at in enumerate(others):
            scale = 1.0 / jnp.sqrt(here * power[y_at] + EPSILON)
            row = LROWS * (1 + 2 * n)
            results.append((total[row : row + LROWS] * scale, total[row + LROWS : row + 2 * LROWS] * scale))
        return results

    def result_copy(u):
        return pltpu.make_async_remote_copy(
            src_ref=mine.at[u],
            dst_ref=theirs.at[u],
            send_sem=res_send.at[u],
            recv_sem=res_recv.at[u],
            device_id=(partner, s),
            device_id_type=MESH,
        )

    def later(u, first_lag, last_lag):
        x_at = OWN0 + u
        lag_list = list(range(first_lag, last_lag + 1))
        results = sums(x_at, [x_at - lag for lag in lag_list])
        for lag, (re_part, im_part) in zip(lag_list, results):
            mine[u - UFIRST, lag - MINLAG, 0] = re_part
            mine[u - UFIRST, lag - MINLAG, 1] = im_part
        result_copy(u - UFIRST).start()

    pass_on(RELAYED[0])

    def pairs_arrived(first, end):
        @pl.loop(first, end)
        def _(i):
            pair_copy(i).wait_recv()

    pairs_arrived(0, MINLAG)

    @pl.loop(0, MINLAG)
    def _(u):
        sums(OWN0 + u, [])

    pairs_arrived(MINLAG, DATES - 1)
    for u in range(MINLAG, MAXLAG):
        if u == DATES - 1:
            pairs_arrived(DATES - 1, DATES)
        later(u, MINLAG, u)
        if u == PASS_AT:
            pass_on(RELAYED[1])

    @pl.loop(MAXLAG, 2 * DATES)
    def _(u):
        later(u, MINLAG, MAXLAG)

    @pl.when(partner_raw)
    def _():
        pair_copy(DATES).wait_recv()

    def back_copy(i):
        return pltpu.make_async_remote_copy(
            src_ref=send_back.at[i, pl.ds(0, MOVED - i)],
            dst_ref=back.at[core, i, pl.ds(0, MOVED - i)],
            send_sem=back_send.at[i],
            recv_sem=back_recv.at[core, i],
            device_id=(2 * chip - 1, s),
            device_id_type=MESH,
        )

    def from_next(i, sent):
        if sent:
            far_arrived(0, i).wait_recv()
        later(2 * DATES + i, max(MINLAG, i + 1), MAXLAG)

    def from_prev(i, sent):
        if sent:
            far_arrived(1, i).wait_recv()
        results = sums(OWN0 - 1 - i, [OWN0 + u for u in range(MOVED, 2 * MOVED - i)])
        for n, (re_part, im_part) in enumerate(results):
            send_back[i, n, 0] = re_part.astype(BF)
            send_back[i, n, 1] = (-im_part).astype(BF)
        back_copy(i).start()

    for i, crossed in enumerate(CROSSED_ORDER):
        pl.when(has_prev & (chip != 4))(functools.partial(from_prev, i, i > 0))
        pl.when(chip == 4)(functools.partial(from_prev, crossed, True))
        pl.when(has_next & (chip != 3))(functools.partial(from_next, i, i > 0))
        pl.when(chip == 3)(functools.partial(from_next, crossed, True))

    @pl.loop(0, 2 * DATES - UFIRST)
    def _(u):
        result_copy(u).wait_recv()

    @pl.when(has_next)
    def _():
        @pl.loop(2 * DATES - UFIRST, UCOUNT)
        def _(u):
            result_copy(u).wait_recv()

    def back_arrived(half, i):
        return pltpu.make_async_remote_copy(
            src_ref=send_back.at[i, pl.ds(0, MOVED - i)],
            dst_ref=back.at[half, i, pl.ds(0, MOVED - i)],
            send_sem=back_send.at[i], recv_sem=back_recv.at[half, i],
            device_id=(partner, s), device_id_type=MESH,
        )

    @pl.when(has_next & (core == 1))
    def _():
        for i in range(MOVED):
            back_arrived(0, i).wait_recv()
            back_arrived(1, i).wait_recv()

    @pl.loop(0, DATES)
    def _(j):
        t = DATES * core + j
        row = jnp.clip(2 * DATES - 1 - t, 0, MOVED - 1)
        for slot in range(4):
            lag = lags[slot, j]
            u = t + lag
            at = jnp.clip(u - UFIRST, 0, UCOUNT - 1)
            which = jnp.clip(lag - MINLAG, 0, LAGS - 1)
            far_at = jnp.clip(u - 2 * DATES - MOVED, 0, MOVED - 1)
            from_back = u >= 2 * DATES + MOVED
            for part in range(2):
                own, got = mine[at, which, part], theirs[at, which, part]
                left = jnp.where(core == 0, own, got)
                right = jnp.where(core == 0, got, own)
                left = jnp.where(from_back, back[0, row, far_at, part].astype(F32), left)
                right = jnp.where(from_back, back[1, row, far_at, part].astype(F32), right)
                value = jnp.concatenate([left, right], axis=1)
                out[j, slot, part] = jnp.where(lag > 0, value, 0.0)

    @pl.loop(0, count)
    def _(i):
        @pl.when(has_down)
        def _():
            edge_copy(None, i, 0).wait_send()

        @pl.when(has_up)
        def _():
            edge_copy(None, i, 1).wait_send()

        pair_copy(i).wait_send()

    @pl.when(has_raw)
    def _():
        for copy in raw_copies():
            copy.wait_send()

    @pl.when(far_ok)
    def _():
        @pl.loop(jnp.where(crossing, 0, 1), MOVED)
        def _(i):
            far_copy(i, 0).wait_send()
            far_copy(i, 1).wait_send()

    @pl.loop(0, 2 * DATES - UFIRST)
    def _(u):
        result_copy(u).wait_send()

    @pl.when(has_next)
    def _():
        @pl.loop(2 * DATES - UFIRST, UCOUNT)
        def _(u):
            result_copy(u).wait_send()

    @pl.when(has_prev)
    def _():
        for i in range(MOVED):
            back_copy(i).wait_send()

    @pl.when(relaying)
    def _():
        for i in RELAYED:
            relay_out(i).wait_send()


def on_device(raw_slc, line_shift, line_phase, col_shift, col_phase, pair_lags):
    smem = pl.BlockSpec(memory_space=pltpu.SMEM)
    dma = pltpu.SemaphoreType.DMA
    part = (2, LROWS, LOOKS)
    return pl.pallas_call(
        kernel,
        out_shape=jax.ShapeDtypeStruct((DATES, 4, 2, LROWS, 2 * LOOKS), F32),
        in_specs=[pl.BlockSpec(memory_space=pl.ANY)] + [smem] * 6,
        out_specs=pl.BlockSpec(memory_space=pltpu.VMEM),
        scratch_shapes=[
            pltpu.VMEM((IMAGES + DATES + 1, ROWS, HALF), BF),
            pltpu.VMEM((len(RELAYED), ROWS, HALF), BF),
            pltpu.VMEM((DATES + 1, 2, EDGE, 2, COLS), BF),
            pltpu.VMEM((LINES, 2, COLS), BF),
            pltpu.SMEM((DATES,), jnp.int32),
            pltpu.SMEM((DATES,), jnp.int32),
            pltpu.SMEM((DATES,), jnp.int32),
            pltpu.SMEM((DATES,), jnp.int32),
            pltpu.SMEM((4,), jnp.int32),
            pltpu.VMEM((2, TILES, SRC, 2, 128), BF),
            pltpu.VMEM((TILES + 5, ROWS, 128), BF),
            pltpu.VMEM((LROWS * (1 + 2 * LAGS), HALF), BF),
            pltpu.VMEM((HALF, LOOKS), BF),
            pltpu.VMEM((IMAGES, LROWS, LOOKS), F32),
            pltpu.VMEM((UCOUNT, LAGS) + part, F32),
            pltpu.VMEM((UCOUNT, LAGS) + part, F32),
            pltpu.VMEM((2, MOVED, MOVED) + part, BF),
            pltpu.VMEM((MOVED, MOVED) + part, BF),
            dma((2,)),
            dma((DATES + 1, 2)),
            dma((DATES + 1, 2)),
            dma((DATES + 1,)),
            dma((DATES + 1,)),
            dma((MOVED, 2)),
            dma((2, MOVED)),
            dma((UCOUNT,)),
            dma((UCOUNT,)),
            dma((MOVED,)),
            dma((2, MOVED)),
            dma((len(RELAYED),)),
            dma((len(RELAYED),)),
            dma((5,)),
            dma((5,)),
        ],
        compiler_params=pltpu.CompilerParams(
            collective_id=0, has_side_effects=True, vmem_limit_bytes=56 * 1024 * 1024
        ),
        name="coherence_stack",
    )(raw_slc, line_shift, line_phase, col_shift, col_phase, pair_lags.T, jnp.asarray(sinc_table()))


def solution(mesh):
    return jax.shard_map(
        on_device,
        mesh=mesh,
        in_specs=(
            P("date", "strip", None, None),
            P("date"),
            P("date"),
            P("date"),
            P("date"),
            P("date", None),
        ),
        out_specs=P("date", None, None, "strip", None),
        check_vma=False,
    )
```
